32 devices in a mesh: groups: 2 (over y), blk: 4 (over x, core), branch: 4 (over z).
Axes of the slice: x: 2, y: 2, z: 4, core: 2. Of those that a mesh axis runs over, the one named last changes fastest.
Arguments:
- queries: bfloat16 [128, 64, 128], P(('groups', 'blk', 'branch')), parts along dimension 0, may hold values from -128 to 128
- new_keys: bfloat16 [128, 8, 128], P(('groups', 'blk', 'branch')), parts along dimension 0, may hold values from -8 to 8
- fresh_token_values: bfloat16 [128, 8, 128], P(('groups', 'blk', 'branch')), parts along dimension 0, may hold values from -6 to 6
- prefix_keys: bfloat16 [16384, 8, 128], P(('groups', 'blk'), 'branch'), parts along dimension 0, may hold values from -4 to 4
- prefix_values: bfloat16 [16384, 8, 128], P(('groups', 'blk'), 'branch'), parts along dimension 0, may hold values from -6 to 6
- suffix_keys: bfloat16 [128, 512, 8, 128], P(('groups', 'blk'), None, 'branch'), parts along dimension 0, may hold values from -8 to 8
- suffix_values: bfloat16 [128, 512, 8, 128], P(('groups', 'blk'), None, 'branch'), parts along dimension 0, may hold values from -6 to 6
- suffix_lengths: int32 [128], P('groups'), parts along dimension 0, may hold values from 1 to 512, 20480 in all
- slot_branch: int32 [128], P('groups'), parts along dimension 0, may hold values from 0 to 63, as said below
Outputs:
- attended: bfloat16 [128, 64, 128], P(('groups', 'blk', 'branch')), parts along dimension 0
The draws below stay inside these ranges and needn't reach their ends.
There are 2 independent parts, one for each index of `groups`. The reference program is written for one: setup_inputs(seed, part) draws one part's arguments, and reference() takes and returns one part's arrays. A program takes and returns all parts, laid end to end along the dimension named above; each array names one. Nothing has to cross between parts.
Inputs may be any that keep to these rules, and one draw needn't show every extreme that they name: slot_branch is a permutation that maps each aligned block of 16 slots onto the branches of the same block of 16 branches.
All inputs are finite; a program needn't handle non-finite values.
Results may differ from the reference program's by a relative error of at most 0.0045.
Values may be sent and summed in bfloat16 or wider, within the bound.
No kernel may reach another device: no remote copies, remote signals or barrier semaphores. Data moves between devices by JAX's collectives and lax.ppermute only.
A program may use at most 128 MiB of HBM per device.

```python
import math
import jax
import jax.numpy as jnp
import numpy as np
from jax import lax

H = 64
KVH = 8
HD = 128
SUF = 512
BR_BLK = 16
BRANCHES = 64
PREFIX = 8192


def prefix_base(key):
    raw_keys = jax.random.normal(jax.random.fold_in(key, 11), (PREFIX, KVH, HD), jnp.float32)
    raw_keys = jnp.clip(raw_keys, -4.0, 4.0)
    return raw_keys


def draw_prefix_keys(key, part):
    return prefix_base(key).astype(jnp.bfloat16)


def draw_queries(key, part):
    sample = jnp.clip(jax.random.normal(jax.random.fold_in(key, 12), (BRANCHES, H, HD), jnp.float32) * 3.0, -12.0, 12.0)
    return sample.astype(jnp.bfloat16)


def draw_slot_branch(key, part):
    block_keys = jax.random.split(jax.random.fold_in(key, 21), BRANCHES // BR_BLK)
    orders = jax.vmap(lambda one_key: jax.random.permutation(one_key, BR_BLK))(block_keys)
    offsets = jnp.arange(BRANCHES // BR_BLK, dtype=jnp.int32)[:, None] * BR_BLK
    return (orders.astype(jnp.int32) + offsets).reshape(BRANCHES).astype(jnp.int32)


def block_levels(stream_key, dims, shards, smallest, largest):
    def one(axis_at, blocks):
        draws = jax.random.uniform(jax.random.fold_in(jax.random.fold_in(stream_key, 6), axis_at), (blocks,), jnp.float32, smallest / len(shards), largest / len(shards))
        return jnp.repeat(jnp.exp(draws), dims[axis_at] // blocks).reshape((-1,) + (1,) * (len(dims) - axis_at - 1))

    level = one(*shards[0])
    for cut in shards[1:]:
        level = level * one(*cut)
    return level


def split_up(number_of, total, most, skew):
    weights = [(1 << 20) // math.isqrt(rank ** skew) + 1 for rank in range(2, number_of + 1)]
    spare, holding = total - most - (number_of - 1), [1] * (number_of - 1)
    while spare > 0:
        free = [i for i in range(number_of - 1) if holding[i] < most]
        mass, remaining = sum([weights[i] for i in free]), spare
        for i in free:
            extra = min(most - holding[i], max(1, remaining * weights[i] // mass), spare)
            holding[i] = holding[i] + extra
            spare = spare - extra
    return np.array([most] + holding)


def uneven_parts(own_key, amount, total, bound, lean):
    if amount == 2:
        one = jax.random.randint(own_key, (), max(1, total - bound), min(bound, total - 1) + 1)
        return jnp.stack([one, total - one])
    lengths = jnp.asarray(split_up(amount, total, bound, lean), jnp.int32)
    pairs = (amount - 1) // 2
    source_of, receiver = lengths[1:1 + 2 * pairs:2], lengths[2:2 + 2 * pairs:2]
    margin = jnp.minimum(source_of - 1, bound - receiver)
    passed = jax.random.randint(jax.random.fold_in(own_key, 1), (pairs,), 0, 1 << 20) % (margin + 1)
    lengths = lengths.at[1:1 + 2 * pairs:2].set(source_of - passed).at[2:2 + 2 * pairs:2].set(receiver + passed)
    return lengths[jax.random.permutation(jax.random.fold_in(own_key, 2), amount)]


def scatter_about(key, dims, scale, limit, cuts=(), kind=jnp.bfloat16):
    drawn = scale * jax.random.normal(key, dims, jnp.float32)
    if cuts:
        drawn = drawn * block_levels(key, dims, cuts, -0.22, 0.18)
    return jnp.clip(drawn, -limit, limit).astype(kind)


def setup_inputs(seed: int = 0, part: int = 0) -> dict:
    splits = jax.random.split(jax.random.key(seed), 10)
    part_keys = jax.random.split(jax.random.fold_in(splits[9], part), 10)
    queries = draw_queries(jax.random.fold_in(jax.random.fold_in(splits[9], part), 71), part)
    new_keys = scatter_about(part_keys[1], (BRANCHES, KVH, HD), 1.7, 8.0, ((0, 16),))
    fresh_token_values = scatter_about(part_keys[2], (BRANCHES, KVH, HD), 1.0, 6.0, ((0, 16),))
    prefix_keys = draw_prefix_keys(jax.random.fold_in(jax.random.fold_in(splits[9], part), 71), part)
    prefix_values = scatter_about(part_keys[4], (PREFIX, KVH, HD), 1.0, 6.0, ((0, 4), (1, 4)))
    suffix_keys = scatter_about(part_keys[5], (BRANCHES, SUF, KVH, HD), 1.3, 8.0, ((0, 4), (2, 4)))
    suffix_values = scatter_about(part_keys[6], (BRANCHES, SUF, KVH, HD), 1.0, 6.0, ((0, 4), (2, 4)))
    suffix_lengths = uneven_parts(part_keys[7], BRANCHES, BRANCHES * SUF * 5 // 8, SUF, 2).astype(jnp.int32)
    slot_branch = draw_slot_branch(jax.random.fold_in(jax.random.fold_in(splits[9], part), 71), part)
    return {"queries": queries, "new_keys": new_keys, "fresh_token_values": fresh_token_values, "prefix_keys": prefix_keys, "prefix_values": prefix_values, "suffix_keys": suffix_keys, "suffix_values": suffix_values, "suffix_lengths": suffix_lengths, "slot_branch": slot_branch}


neg_large = -1e+30

def advance(carried, scores, apply_values):
    out_sum, top_score, weight_sum = carried
    new_top = jnp.maximum(top_score, lax.optimization_barrier(jnp.max(scores, axis=-1)))
    rescale = jnp.exp(top_score - new_top)
    weights = jnp.exp(scores - new_top[..., None])
    weight_sum = weight_sum * rescale + lax.optimization_barrier(jnp.sum(weights, axis=-1))
    rounded = lax.optimization_barrier(weights.astype(jnp.bfloat16))
    out_sum = out_sum * rescale[..., None] + apply_values(rounded.astype(jnp.float32))
    return (out_sum, new_top, weight_sum)

def combine(first, second):
    top_score = jnp.maximum(first[1], second[1])
    scale_one = jnp.exp(first[1] - top_score)
    scale_two = jnp.exp(second[1] - top_score)
    out_sum = first[0] * scale_one[..., None] + second[0] * scale_two[..., None]
    weight_sum = first[2] * scale_one + second[2] * scale_two
    return (out_sum, top_score, weight_sum)

def prefix_part(grouped, prefix_keys, prefix_values, score_scale):
    rows, kv_heads, group, head_dim = grouped.shape
    total = prefix_keys.shape[0]
    width = math.gcd(total, 512)
    count = total // width
    query_wide = grouped.astype(jnp.float32)
    key_blocks = prefix_keys.reshape(count, width, kv_heads, head_dim)
    value_blocks = prefix_values.reshape(count, width, kv_heads, head_dim)
    initial = (jnp.zeros((rows, kv_heads, group, head_dim), jnp.float32), jnp.full((rows, kv_heads, group), neg_large, jnp.float32), jnp.zeros((rows, kv_heads, group), jnp.float32))

    def step(carried, blocks):
        key_block, value_block = blocks
        scores = jnp.einsum('rkgd,nkd->rkgn', query_wide, key_block.astype(jnp.float32)) * score_scale

        def apply_values(weights):
            return jnp.einsum('rkgn,nkd->rkgd', weights, value_block.astype(jnp.float32))
        return (advance(carried, scores, apply_values), None)
    final_output, _ = lax.scan(step, initial, (key_blocks, value_blocks))
    return final_output

def suffix_block(arrays, score_scale):
    slot_queries, slot_new_keys, slot_new_values, branch_slot_keys, slot_values, slot_lengths = arrays
    query_wide = slot_queries.astype(jnp.float32)
    group = slot_queries.shape[2]
    own_score = jnp.einsum('skgd,skd->skg', query_wide, slot_new_keys.astype(jnp.float32)) * score_scale
    own_value = jnp.broadcast_to(slot_new_values.astype(jnp.float32)[:, :, None, :], slot_queries.shape)
    carried = (own_value, own_score, jnp.ones_like(own_score))
    scores = jnp.einsum('skgd,snkd->skgn', query_wide, branch_slot_keys.astype(jnp.float32)) * score_scale
    positions = jnp.arange(branch_slot_keys.shape[1], dtype=jnp.int32)
    valid_mask = positions[None, :] < slot_lengths[:, None]
    scores = jnp.where(valid_mask[:, None, None, :], scores, neg_large)
    values_wide = slot_values.astype(jnp.float32)

    def apply_values(weights):
        return jnp.einsum('skgn,snkd->skgd', weights, values_wide)
    return advance(carried, scores, apply_values)

def reference(queries, new_keys, fresh_token_values, prefix_keys, prefix_values, suffix_keys, suffix_values, suffix_lengths, slot_branch):
    group = H // KVH
    score_scale = 1.0 / math.sqrt(HD)
    grouped = queries.reshape(BRANCHES, KVH, group, HD)
    prefix_state = prefix_part(grouped, prefix_keys, prefix_values, score_scale)
    slot_arrays = (grouped[slot_branch], new_keys[slot_branch], fresh_token_values[slot_branch], suffix_keys, suffix_values, suffix_lengths[slot_branch])
    width = math.gcd(BRANCHES, 64)
    count = BRANCHES // width
    stacked = tuple((item.reshape((count, width) + item.shape[1:]) for item in slot_arrays))
    slot_state = lax.map(lambda arrays: suffix_block(arrays, score_scale), stacked)
    slot_state = tuple((member.reshape((BRANCHES,) + member.shape[2:]) for member in slot_state))
    slot_of = jnp.zeros((BRANCHES,), jnp.int32).at[slot_branch].set(jnp.arange(BRANCHES, dtype=jnp.int32))
    suffix_state = tuple((member[slot_of] for member in slot_state))
    out_sum, top_score, weight_sum = combine(prefix_state, suffix_state)
    final_output = (out_sum / weight_sum[..., None]).astype(jnp.bfloat16)
    return final_output.reshape(BRANCHES, H, HD)
```

```python
import functools
import math

import jax
import jax.numpy as jnp
from jax import lax
from jax.experimental import pallas as pl
from jax.experimental.pallas import tpu as pltpu
from jax.sharding import PartitionSpec as P

NEG = -1e30
LOG2E = 1.4426950408889634
F32 = jnp.float32
BF16 = jnp.bfloat16
VM = pl.BlockSpec(memory_space=pltpu.VMEM)
SM = pl.BlockSpec(memory_space=pltpu.SMEM)
ANY = pl.BlockSpec(memory_space=pl.ANY)
NT = (((1,), (1,)), ((), ()))


def ceil_to(value, unit):
    return -(-value // unit) * unit


def partner(index, step, count):
    if count & (count - 1) == 0:
        return index ^ step
    return (index + step) % count


def back(step, count):
    return step if count & (count - 1) == 0 else (count - step) % count


def step_to(me, other, count):
    if count & (count - 1) == 0:
        return me ^ other
    return lax.rem(me - other + count, count)


def call(kernel, name, out_shape, inputs, in_specs, scratch=(), vmem=16 << 20, flops=0, moved=0, out_specs=None):
    many = isinstance(out_shape, (list, tuple))
    return pl.pallas_call(
        kernel,
        name=name,
        out_shape=out_shape,
        in_specs=in_specs,
        out_specs=out_specs if out_specs is not None else ([VM] * len(out_shape) if many else VM),
        scratch_shapes=list(scratch),
        compiler_params=pltpu.CompilerParams(vmem_limit_bytes=vmem),
        cost_estimate=pl.CostEstimate(flops=flops, bytes_accessed=moved, transcendentals=0),
    )(*inputs)


def pack_kernel(nz, local, group, pad, q_ref, k_ref, v_ref, *out_refs):
    me = lax.axis_index("branch")
    nb = q_ref.shape[0]
    head_dim = q_ref.shape[-1]
    new_k = k_ref[...].astype(F32)
    new_v = v_ref[...].astype(F32)
    for step in range(nz):
        peer = partner(me, step, nz)
        q = q_ref[:, peer].astype(F32)
        parts = [
            q[:, kl * group : (kl + 1) * group].reshape(nb * group, head_dim) for kl in range(local)
        ]
        rows_k, rows_v = new_k[:, :local], new_v[:, :local]
        for z in range(1, nz):
            here = peer == z
            rows_k = jnp.where(here, new_k[:, z * local : (z + 1) * local], rows_k)
            rows_v = jnp.where(here, new_v[:, z * local : (z + 1) * local], rows_v)
        for rows in (rows_k, rows_v):
            for kl in range(local):
                parts += [rows[b, kl : kl + 1] for b in range(nb)]
        if pad:
            parts.append(jnp.zeros((pad, head_dim), F32))
        out_refs[step][...] = jnp.concatenate(parts, axis=0).astype(BF16)


def join_kernel(*refs):
    for step, ref in enumerate(refs[:-1]):
        refs[-1][step] = ref[...]


def split_kernel(local, k_ref, v_ref, ko_ref, vo_ref, wide):
    chunk = wide.shape[0]
    rows = chunk // local
    for src, dst in ((k_ref, ko_ref), (v_ref, vo_ref)):
        for at in range(src.shape[0] // chunk):
            wide[...] = src[at * chunk : (at + 1) * chunk].astype(F32)
            for kl in range(local):
                dst[kl, at * rows : (at + 1) * rows] = wide[pl.ds(kl, rows, stride=local)].astype(BF16)


def suffix_kernel(
    nz, local, group, scale, joined_ref, slot_ref, len_ref, keys, values, out_ref, lse_ref,
    kbuf, vbuf, qwide, scores, probs, ksem, vsem
):
    slots, width, head_dim = kbuf.shape
    block = lax.axis_index("blk")
    me = lax.axis_index("branch")
    copies_k = [pltpu.make_async_copy(keys.at[c], kbuf.at[c], ksem.at[c]) for c in range(slots)]
    copies_v = [pltpu.make_async_copy(values.at[c], vbuf.at[c], vsem.at[c]) for c in range(slots)]
    for copy in copies_k + copies_v:
        copy.start()
    nb = slots // nz
    qrows = local * nb * group
    for step in range(nz):
        qwide[step * qrows : (step + 1) * qrows] = joined_ref[step, :qrows].astype(F32)
    heads = local * group
    column = lax.broadcasted_iota(jnp.int32, (heads, width), 1)
    row = lax.broadcasted_iota(jnp.int32, (heads, width), 0)
    own_head = lax.rem(column, local) == row // group

    def places(c):
        branch = slot_ref[block * slots + c]
        length = len_ref[branch]
        branch = branch - block * slots
        step = step_to(me, branch // nb, nz)
        at = step * qrows + lax.rem(branch, nb) * group
        return [pl.multiple_of(at + kl * nb * group, 8) for kl in range(local)], length

    for c in range(slots):
        at, length = places(c)
        q = jnp.concatenate([qwide[pl.ds(a, group)] for a in at], axis=0).astype(BF16)
        copies_k[c].wait()
        s = lax.dot_general(q, kbuf[c], NT, preferred_element_type=F32)
        scores[c * heads : (c + 1) * heads] = jnp.where(
            own_head & (column < length * local), s, NEG
        )
    s = scores[...]
    top = jnp.max(s, axis=-1, keepdims=True)
    weights = jnp.exp2((s - top) * (scale * LOG2E))
    total = jnp.sum(weights, axis=-1, keepdims=True)
    probs[...] = weights.astype(BF16)
    lse = top * scale + jnp.log(total)
    inverse = 1.0 / total
    for c in range(slots):
        at, _ = places(c)
        copies_v[c].wait()
        o = jnp.dot(probs[c * heads : (c + 1) * heads], vbuf[c], preferred_element_type=F32)
        o = o * inverse[c * heads : (c + 1) * heads]
        for kl in range(local):
            lo, hi = kl * group, (kl + 1) * group
            out_ref[pl.ds(at[kl], group)] = o[lo:hi]
            lse_ref[pl.ds(at[kl], group)] = jnp.broadcast_to(
                lse[c * heads + lo : c * heads + hi], (group, head_dim)
            )


def column_to_rows(column, lanes):
    count = column.shape[0] // lanes
    eye = lax.broadcasted_iota(jnp.int32, (lanes, lanes), 0) == lax.broadcasted_iota(
        jnp.int32, (lanes, lanes), 1
    )
    rows = [
        jnp.sum(jnp.where(eye, column[i * lanes : (i + 1) * lanes], 0.0), axis=0, keepdims=True)
        for i in range(count)
    ]
    return jnp.concatenate(rows, axis=0)


def rows_to_column(rows):
    lanes = rows.shape[1]
    eye = lax.broadcasted_iota(jnp.int32, (lanes, lanes), 0) == lax.broadcasted_iota(
        jnp.int32, (lanes, lanes), 1
    )
    parts = [
        jnp.sum(jnp.where(eye, rows[i : i + 1], 0.0), axis=1, keepdims=True)
        for i in range(rows.shape[0])
    ]
    return jnp.concatenate(parts, axis=0)


def encode(out, lse):
    lanes = out.shape[1]
    rows = column_to_rows(lse, lanes)
    high = rows.astype(BF16).astype(F32)
    middle = (rows - high).astype(BF16).astype(F32)
    low = rows - high - middle
    tail = [high, middle, low]
    used = 3 * rows.shape[0]
    tail.append(jnp.zeros((ceil_to(used, 16) - used, lanes), F32))
    return jnp.concatenate([out] + tail, axis=0).astype(BF16)


def decode(payload, count):
    wide = payload.astype(F32)
    lanes = wide.shape[1]
    n = count // lanes
    rows = wide[count : count + n] + wide[count + n : count + 2 * n] + wide[count + 2 * n : count + 3 * n]
    return wide[:count], rows_to_column(rows)


def merge(parts):
    top = parts[0][1]
    for _, lse in parts[1:]:
        top = jnp.maximum(top, lse)
    weights = [jnp.exp2((lse - top) * LOG2E) for _, lse in parts]
    total = sum(weights[1:], weights[0])
    out = parts[0][0] * weights[0]
    for (o, _), w in zip(parts[1:], weights[1:]):
        out = out + o * w
    return out * (1.0 / total), top + jnp.log(total)


def prefix_partial(q_refs, k_ref, v_ref, local, qrows, scale):
    part = qrows // local
    steps = q_refs[0].shape[0]
    outs, lses = [], []
    for kl in range(local):
        q = jnp.concatenate(
            [ref[z, kl * part : (kl + 1) * part] for ref in q_refs for z in range(steps)], axis=0
        )
        s = lax.dot_general(q, k_ref[kl], NT, preferred_element_type=F32)
        top = jnp.max(s, axis=-1, keepdims=True)
        weights = jnp.exp2((s - top) * (scale * LOG2E))
        total = jnp.sum(weights, axis=-1, keepdims=True)
        o = jnp.dot(weights.astype(BF16), v_ref[kl], preferred_element_type=F32)
        outs.append(o * (1.0 / total))
        lses.append(top * scale + jnp.log(total))
    results = []
    for i in range(len(q_refs)):
        pieces = [(i * steps + z) * part for z in range(steps)]
        results.append(
            tuple(
                jnp.concatenate([a[p : p + part] for p in pieces for a in arrays], axis=0)
                for arrays in (outs, lses)
            )
        )
    return results


def prefix_kernel(count, merged, local, qrows, scale, *refs):
    q_refs, (k_ref, v_ref) = refs[:count], refs[count : count + 2]
    others = refs[count + 2 : count + 2 + (count if merged else 0)]
    outs = refs[-count:]
    results = prefix_partial(q_refs, k_ref, v_ref, local, qrows, scale)
    for i, (o, lse) in enumerate(results):
        if merged:
            o, lse = merge([(o, lse), decode(others[i][...], o.shape[0])])
        outs[i][...] = encode(o, lse)


def prefix_own_kernel(local, qrows, scale, q_ref, k_ref, v_ref, o_ref, lse_ref):
    ((o, lse),) = prefix_partial([q_ref], k_ref, v_ref, local, qrows, scale)
    o_ref[...] = o
    lse_ref[...] = jnp.broadcast_to(lse, o.shape)


def final_kernel(count, local, group, scale, joined_ref, so_ref, sl_ref, po_ref, pl_ref, *refs):
    others, outs = refs[:count], refs[count:]
    nz = joined_ref.shape[0]
    rows, head_dim = po_ref.shape
    qrows = rows // nz
    nb = qrows // (local * group)
    part = nb * local
    own_score, own_value = [], []
    for step in range(nz):
        q = joined_ref[step, :qrows].astype(F32)
        tail = joined_ref[step, qrows:].astype(F32)
        k = jnp.concatenate(
            [jnp.broadcast_to(tail[i : i + 1], (group, head_dim)) for i in range(part)], axis=0
        )
        own_value += [
            jnp.broadcast_to(tail[i : i + 1], (group, head_dim)) for i in range(part, 2 * part)
        ]
        own_score.append(jnp.sum(q * k, axis=1, keepdims=True) * scale)
    parts = [
        (jnp.concatenate(own_value, axis=0), jnp.concatenate(own_score, axis=0)),
        (so_ref[...], sl_ref[:, :1]),
        (po_ref[...], pl_ref[:, :1]),
    ]
    parts += [decode(ref[...], rows) for ref in others]
    out, _ = merge(parts)
    for step in range(nz):
        outs[step][...] = out[step * qrows : (step + 1) * qrows].astype(BF16)


def unpack_kernel(nz, local, group, *refs):
    pieces, out_ref = refs[:nz], refs[nz]
    me = lax.axis_index("branch")
    nb = out_ref.shape[0]
    for step in range(nz):
        peer = partner(me, step, nz)
        wide = pieces[step][...].astype(F32)
        for b in range(nb):
            rows = [wide[(kl * nb + b) * group : (kl * nb + b + 1) * group] for kl in range(local)]
            out_ref[b, peer] = jnp.concatenate(rows, axis=0).astype(BF16)


def per_device(
    nz, nblk, queries, new_keys, fresh_token_values, prefix_keys, prefix_values, suffix_keys,
    suffix_values, suffix_lengths, slot_branch
):
    nb, heads, head_dim = queries.shape
    positions, local = prefix_keys.shape[:2]
    group = heads // new_keys.shape[1]
    slots, suffix = suffix_keys.shape[:2]
    scale = 1.0 / math.sqrt(head_dim)
    qrows = local * nb * group
    used = qrows + 2 * nb * local
    padded = ceil_to(used, 16)
    rows = nz * qrows
    nc = 2 if nblk % 2 == 0 else 1
    nx = nblk // nc

    def shift(x, axis, step, count, unit=1, size=None):
        size = count * unit if size is None else size
        pairs = []
        for i in range(size):
            inner, outer = i % unit, i // unit
            low = outer % count
            other = outer - low + partner(low, step, count)
            pairs.append((i, other * unit + inner))
        return lax.ppermute(x, axis, pairs)

    def along_core(x):
        return shift(x, "blk", 1, 2, 1, nblk)

    def along_x(x, step):
        return shift(x, "blk", step, nx, nc, nblk)

    payloads = call(
        functools.partial(pack_kernel, nz, local, group, padded - used),
        "pack",
        [jax.ShapeDtypeStruct((padded, head_dim), BF16)] * nz,
        (queries.reshape(nb, nz, heads // nz, head_dim), new_keys, fresh_token_values),
        [VM] * 3,
        moved=queries.size * 4,
    )
    arrived = [payloads[0]] + [
        shift(payloads[step], "branch", step, nz) for step in range(nz - 1, 0, -1)
    ][::-1]
    if local > 1:
        chunk = math.gcd(positions * local, 1024)
        flat = (positions * local, head_dim)
        keys, values = call(
            functools.partial(split_kernel, local),
            "split",
            [jax.ShapeDtypeStruct((local, positions, head_dim), BF16)] * 2,
            (prefix_keys.reshape(flat), prefix_values.reshape(flat)),
            [VM] * 2,
            scratch=[pltpu.VMEM((chunk, head_dim), F32)],
            moved=prefix_keys.size * 8,
        )
    else:
        keys = prefix_keys.reshape(1, positions, head_dim)
        values = prefix_values.reshape(1, positions, head_dim)
    joined = call(
        join_kernel,
        "join",
        jax.ShapeDtypeStruct((nz, padded, head_dim), BF16),
        arrived,
        [VM] * nz,
        moved=nz * padded * head_dim * 4,
    )

    def prefix(name, arrays, others=()):
        count = len(arrays)
        return call(
            functools.partial(prefix_kernel, count, bool(others), local, qrows, scale),
            name,
            [jax.ShapeDtypeStruct((rows + ceil_to(3 * (rows // head_dim), 16), head_dim), BF16)] * count,
            (*arrays, keys, values, *others),
            [VM] * (count + 2 + len(others)),
            vmem=48 << 20,
            flops=4 * count * rows * positions * head_dim,
            moved=keys.size * 4,
        )

    far = {step: along_x(joined, step) for step in range(1, nx)}
    near = along_core(joined) if nc > 1 else None
    far_near = {step: along_core(far[step]) for step in far} if nc > 1 else {}

    width = suffix * local
    suffix_out, suffix_lse = call(
        functools.partial(suffix_kernel, nz, local, group, scale),
        "suffix",
        [jax.ShapeDtypeStruct((rows, head_dim), F32)] * 2,
        (
            joined, slot_branch, suffix_lengths,
            suffix_keys.reshape(slots, width, head_dim), suffix_values.reshape(slots, width, head_dim),
        ),
        [VM, SM, SM, ANY, ANY],
        scratch=[
            pltpu.VMEM((slots, width, head_dim), BF16),
            pltpu.VMEM((slots, width, head_dim), BF16),
            pltpu.VMEM((rows, head_dim), F32),
            pltpu.VMEM((slots * local * group, width), F32),
            pltpu.VMEM((slots * local * group, width), BF16),
            pltpu.SemaphoreType.DMA((slots,)),
            pltpu.SemaphoreType.DMA((slots,)),
        ],
        vmem=32 << 20,
        flops=4 * rows * width * head_dim,
        moved=suffix_keys.size * 4,
    )
    received = []
    merged = {}
    if nc > 1:
        sent = prefix("prefix_sibling", [near] + [far_near[step] for step in far])
        got = [along_core(x) for x in sent]
        received.append(got[0])
        merged = dict(zip(far, got[1:]))
    own_out, own_lse = call(
        functools.partial(prefix_own_kernel, local, qrows, scale),
        "prefix_own",
        [jax.ShapeDtypeStruct((rows, head_dim), F32)] * 2,
        (joined, keys, values),
        [VM] * 3,
        vmem=48 << 20,
        flops=4 * rows * positions * head_dim,
        moved=keys.size * 4,
    )
    if far:
        sent = prefix("prefix_far", list(far.values()), [merged[step] for step in far] if nc > 1 else ())
        received += [along_x(x, back(step, nx)) for x, step in zip(sent, far)]
    pieces = call(
        functools.partial(final_kernel, len(received), local, group, scale),
        "final",
        [jax.ShapeDtypeStruct((qrows, head_dim), BF16)] * nz,
        (joined, suffix_out, suffix_lse, own_out, own_lse, *received),
        [VM] * (5 + len(received)),
        moved=rows * head_dim * 20,
    )
    landed = [pieces[0]] + [
        shift(pieces[step], "branch", back(step, nz), nz) for step in range(nz - 1, 0, -1)
    ][::-1]
    out = call(
        functools.partial(unpack_kernel, nz, local, group),
        "unpack",
        jax.ShapeDtypeStruct((nb, nz, heads // nz, head_dim), BF16),
        landed,
        [VM] * nz,
        moved=queries.size * 4,
    )
    return out.reshape(nb, heads, head_dim)


def solution(mesh):
    lanes = P(("groups", "blk", "branch"), None, None)
    return jax.shard_map(
        functools.partial(per_device, mesh.shape["branch"], mesh.shape["blk"]),
        mesh=mesh,
        in_specs=(
            lanes,
            lanes,
            lanes,
            P(("groups", "blk"), "branch", None),
            P(("groups", "blk"), "branch", None),
            P(("groups", "blk"), None, "branch", None),
            P(("groups", "blk"), None, "branch", None),
            P("groups"),
            P("groups"),
        ),
        out_specs=lanes,
        check_vma=False,
    )
```

```python
import functools
import math

import jax
import jax.numpy as jnp
from jax import lax
from jax.experimental import pallas as pl
from jax.experimental.pallas import tpu as pltpu
from jax.sharding import PartitionSpec as P

NEG = -1e30
GAP = 1 << 36
LOG2E = 1.4426950408889634
F32 = jnp.float32
BF16 = jnp.bfloat16
VM = pl.BlockSpec(memory_space=pltpu.VMEM)
SM = pl.BlockSpec(memory_space=pltpu.SMEM)
HBM = pl.BlockSpec(memory_space=pltpu.HBM)
NT = (((1,), (1,)), ((), ()))


def ceil_to(value, unit):
    return -(-value // unit) * unit


def partner(index, step, count):
    if count & (count - 1) == 0:
        return index ^ step
    return (index + step) % count


def back(step, count):
    return step if count & (count - 1) == 0 else (count - step) % count


def step_to(me, other, count):
    if count & (count - 1) == 0:
        return me ^ other
    return lax.rem(me - other + count, count)


def in_hbm(x):
    return pltpu.with_memory_space_constraint(x, pltpu.HBM)


def call(kernel, name, out_shape, inputs, in_specs, scratch=(), vmem=16 << 20, flops=0, moved=0, out_specs=None):
    many = isinstance(out_shape, (list, tuple))
    return pl.pallas_call(
        kernel,
        name=name,
        out_shape=out_shape,
        in_specs=in_specs,
        out_specs=out_specs if out_specs is not None else ([VM] * len(out_shape) if many else VM),
        scratch_shapes=list(scratch),
        compiler_params=pltpu.CompilerParams(vmem_limit_bytes=vmem),
        cost_estimate=pl.CostEstimate(flops=flops, bytes_accessed=moved, transcendentals=0),
    )(*inputs)


def pack_kernel(nz, local, group, pad, q_hbm, k_hbm, v_hbm, *refs):
    out_refs, (q_ref, k_ref, v_ref, sems) = refs[:nz], refs[nz:]
    copies = [
        pltpu.make_async_copy(src, dst, sems.at[i])
        for i, (src, dst) in enumerate(((q_hbm, q_ref), (k_hbm, k_ref), (v_hbm, v_ref)))
    ]
    for copy in copies:
        copy.start()
    for copy in copies:
        copy.wait()
    me = lax.axis_index("branch")
    nb = q_ref.shape[0]
    head_dim = q_ref.shape[-1]
    new_k = k_ref[...].astype(F32)
    new_v = v_ref[...].astype(F32)
    for step in range(nz):
        peer = partner(me, step, nz)
        q = q_ref[:, peer].astype(F32)
        parts = [
            q[:, kl * group : (kl + 1) * group].reshape(nb * group, head_dim) for kl in range(local)
        ]
        rows_k, rows_v = new_k[:, :local], new_v[:, :local]
        for z in range(1, nz):
            here = peer == z
            rows_k = jnp.where(here, new_k[:, z * local : (z + 1) * local], rows_k)
            rows_v = jnp.where(here, new_v[:, z * local : (z + 1) * local], rows_v)
        for rows in (rows_k, rows_v):
            for kl in range(local):
                parts += [rows[b, kl : kl + 1] for b in range(nb)]
        if pad:
            parts.append(jnp.zeros((pad, head_dim), F32))
        out_refs[step][...] = jnp.concatenate(parts, axis=0).astype(BF16)


def join_kernel(nz, qrows, *refs):
    q_ref, tail_ref = refs[-2:]
    for step in range(nz):
        q_ref[step] = refs[nz - 1 - step][:qrows]
        tail_ref[step] = refs[nz - 1 - step][qrows:]


def gap_kernel(after, token):
    token[...] = jnp.zeros(token.shape, token.dtype)


def split_kernel(local, pk, pv, pko, pvo, token, wide):
    token[...] = jnp.zeros(token.shape, token.dtype)
    chunk = wide.shape[0]
    rows = chunk // local
    for src, dst in ((pk, pko), (pv, pvo)):
        for at in range(src.shape[0] // chunk):
            if local == 1:
                dst[0, at * rows : (at + 1) * rows] = src[at * chunk : (at + 1) * chunk]
                continue
            wide[...] = src[at * chunk : (at + 1) * chunk].astype(F32)
            for kl in range(local):
                dst[kl, at * rows : (at + 1) * rows] = wide[pl.ds(kl, rows, stride=local)].astype(BF16)


def suffix_kernel(
    nz, local, group, scale, joined_ref, slot_ref, len_ref, keys, values, out_ref, lse_ref,
    qwide, scores, probs
):
    slots, width, head_dim = keys.shape
    block = lax.axis_index("blk")
    me = lax.axis_index("branch")
    nb = slots // nz
    qrows = local * nb * group
    for step in range(nz):
        qwide[step * qrows : (step + 1) * qrows] = joined_ref[step, :qrows].astype(F32)
    heads = local * group
    column = lax.broadcasted_iota(jnp.int32, (heads, width), 1)
    row = lax.broadcasted_iota(jnp.int32, (heads, width), 0)
    own_head = lax.rem(column, local) == row // group

    def places(c):
        branch = slot_ref[block * slots + c]
        length = len_ref[branch]
        branch = branch - block * slots
        step = step_to(me, branch // nb, nz)
        at = step * qrows + lax.rem(branch, nb) * group
        return [pl.multiple_of(at + kl * nb * group, 8) for kl in range(local)], length

    for c in range(slots):
        at, length = places(c)
        q = jnp.concatenate([qwide[pl.ds(a, group)] for a in at], axis=0).astype(BF16)
        s = lax.dot_general(q, keys[c], NT, preferred_element_type=F32)
        scores[c * heads : (c + 1) * heads] = jnp.where(
            own_head & (column < length * local), s, NEG
        )
    s = scores[...]
    top = jnp.max(s, axis=-1, keepdims=True)
    weights = jnp.exp2((s - top) * (scale * LOG2E))
    total = jnp.sum(weights, axis=-1, keepdims=True)
    probs[...] = weights.astype(BF16)
    lse = top * scale + jnp.log(total)
    inverse = 1.0 / total
    for c in range(slots):
        at, _ = places(c)
        o = jnp.dot(probs[c * heads : (c + 1) * heads], values[c], preferred_element_type=F32)
        o = o * inverse[c * heads : (c + 1) * heads]
        for kl in range(local):
            lo, hi = kl * group, (kl + 1) * group
            out_ref[pl.ds(at[kl], group)] = o[lo:hi]
            lse_ref[pl.ds(at[kl], group)] = jnp.broadcast_to(
                lse[c * heads + lo : c * heads + hi], (group, head_dim)
            )


def column_to_rows(column, lanes):
    count = column.shape[0] // lanes
    eye = lax.broadcasted_iota(jnp.int32, (lanes, lanes), 0) == lax.broadcasted_iota(
        jnp.int32, (lanes, lanes), 1
    )
    rows = [
        jnp.sum(jnp.where(eye, column[i * lanes : (i + 1) * lanes], 0.0), axis=0, keepdims=True)
        for i in range(count)
    ]
    return jnp.concatenate(rows, axis=0)


def rows_to_column(rows):
    lanes = rows.shape[1]
    eye = lax.broadcasted_iota(jnp.int32, (lanes, lanes), 0) == lax.broadcasted_iota(
        jnp.int32, (lanes, lanes), 1
    )
    parts = [
        jnp.sum(jnp.where(eye, rows[i : i + 1], 0.0), axis=1, keepdims=True)
        for i in range(rows.shape[0])
    ]
    return jnp.concatenate(parts, axis=0)


def encode(out, lse):
    lanes = out.shape[1]
    rows = column_to_rows(lse, lanes)
    high = rows.astype(BF16).astype(F32)
    middle = (rows - high).astype(BF16).astype(F32)
    low = rows - high - middle
    tail = [high, middle, low]
    used = 3 * rows.shape[0]
    tail.append(jnp.zeros((ceil_to(used, 16) - used, lanes), F32))
    return jnp.concatenate([out] + tail, axis=0).astype(BF16)


def decode(payload, count):
    wide = payload.astype(F32)
    lanes = wide.shape[1]
    n = count // lanes
    rows = wide[count : count + n] + wide[count + n : count + 2 * n] + wide[count + 2 * n : count + 3 * n]
    return wide[:count], rows_to_column(rows)


def merge(parts):
    top = parts[0][1]
    for _, lse in parts[1:]:
        top = jnp.maximum(top, lse)
    weights = [jnp.exp2((lse - top) * LOG2E) for _, lse in parts]
    total = sum(weights[1:], weights[0])
    out = parts[0][0] * weights[0]
    for (o, _), w in zip(parts[1:], weights[1:]):
        out = out + o * w
    return out * (1.0 / total), top + jnp.log(total)


def prefix_partial(q_refs, k_ref, v_ref, local, qrows, scale):
    part = qrows // local
    steps = q_refs[0].shape[0]
    outs, lses = [], []
    for kl in range(local):
        q = jnp.concatenate(
            [ref[z, kl * part : (kl + 1) * part] for ref in q_refs for z in range(steps)], axis=0
        )
        s = lax.dot_general(q, k_ref[kl], NT, preferred_element_type=F32)
        top = jnp.max(s, axis=-1, keepdims=True)
        weights = jnp.exp2((s - top) * (scale * LOG2E))
        total = jnp.sum(weights, axis=-1, keepdims=True)
        o = jnp.dot(weights.astype(BF16), v_ref[kl], preferred_element_type=F32)
        outs.append(o * (1.0 / total))
        lses.append(top * scale + jnp.log(total))
    results = []
    for i in range(len(q_refs)):
        pieces = [(i * steps + z) * part for z in range(steps)]
        results.append(
            tuple(
                jnp.concatenate([a[p : p + part] for p in pieces for a in arrays], axis=0)
                for arrays in (outs, lses)
            )
        )
    return results


def prefix_kernel(count, *refs, local, qrows, scale):
    q_refs, (k_ref, v_ref), outs = refs[:count], refs[count : count + 2], refs[count + 2 :]
    for ref, (o, lse) in zip(outs, prefix_partial(q_refs, k_ref, v_ref, local, qrows, scale)):
        ref[...] = encode(o, lse)


def prefix_own_kernel(q_ref, k_ref, v_ref, o_ref, lse_ref, *, local, qrows, scale):
    ((o, lse),) = prefix_partial([q_ref], k_ref, v_ref, local, qrows, scale)
    o_ref[...] = o
    lse_ref[...] = jnp.broadcast_to(lse, o.shape)


def near_kernel(count, local, group, scale, q_ref, fresh_ref, so_ref, sl_ref, po_ref, pl_ref, *refs):
    others, (out_ref, lse_ref) = refs[:count], refs[count:]
    rows, head_dim = po_ref.shape
    nz, qrows = q_ref.shape[:2]
    part = qrows // group
    own_score, own_value = [], []
    for step in range(nz):
        q = q_ref[step].astype(F32)
        tail = fresh_ref[step].astype(F32)
        k, v = (
            jnp.concatenate(
                [jnp.broadcast_to(tail[i : i + 1], (group, head_dim)) for i in range(at, at + part)],
                axis=0,
            )
            for at in (0, part)
        )
        own_score.append(jnp.sum(q * k, axis=1, keepdims=True) * scale)
        own_value.append(v)
    parts = [
        (jnp.concatenate(own_value, axis=0), jnp.concatenate(own_score, axis=0)),
        (so_ref[...], sl_ref[:, :1]),
        (po_ref[...], pl_ref[:, :1]),
    ]
    parts += [decode(ref[...], rows) for ref in others]
    out, lse = merge(parts)
    out_ref[...] = out
    lse_ref[...] = jnp.broadcast_to(lse, out.shape)


def final_kernel(count, near_ref, lse_ref, *refs):
    others, outs = refs[:count], refs[count:]
    parts = [(near_ref[...], lse_ref[:, :1])]
    parts += [decode(ref[...], near_ref.shape[0]) for ref in others]
    out, _ = merge(parts)
    qrows = outs[0].shape[0]
    for step, ref in enumerate(outs):
        ref[...] = out[step * qrows : (step + 1) * qrows].astype(BF16)


def unpack_kernel(nz, local, group, *refs):
    pieces, out_ref = refs[:nz], refs[nz]
    me = lax.axis_index("branch")
    nb = out_ref.shape[0]
    for step in range(nz):
        peer = partner(me, step, nz)
        wide = pieces[nz - 1 - step][...].astype(F32)
        for b in range(nb):
            rows = [wide[(kl * nb + b) * group : (kl * nb + b + 1) * group] for kl in range(local)]
            out_ref[b, peer] = jnp.concatenate(rows, axis=0).astype(BF16)


def per_device(
    nz, nblk, queries, new_keys, fresh_token_values, prefix_keys, prefix_values, suffix_keys,
    suffix_values, suffix_lengths, slot_branch
):
    nb, heads, head_dim = queries.shape
    positions, local = prefix_keys.shape[:2]
    group = heads // new_keys.shape[1]
    slots, suffix = suffix_keys.shape[:2]
    scale = 1.0 / math.sqrt(head_dim)
    qrows = local * nb * group
    used = qrows + 2 * nb * local
    padded = ceil_to(used, 16)
    rows = nz * qrows
    nc = 2 if nblk % 2 == 0 else 1
    nx = nblk // nc

    def shift(x, axis, step, count):
        return lax.ppermute(x, axis, [(i, partner(i, step, count)) for i in range(count)])

    def along_blk(x, step_x, step_c):
        return lax.ppermute(
            x,
            "blk",
            [
                (i, partner(i // nc, step_x, nx) * nc + partner(i % nc, step_c, nc))
                for i in range(nblk)
            ],
        )

    payloads = call(
        functools.partial(pack_kernel, nz, local, group, padded - used),
        "pack",
        [pltpu.VMEM((padded, head_dim), BF16)] * nz,
        (
            in_hbm(queries.reshape(nb, nz, heads // nz, head_dim)),
            in_hbm(new_keys), in_hbm(fresh_token_values),
        ),
        [HBM] * 3,
        scratch=[
            pltpu.VMEM((nb, nz, heads // nz, head_dim), BF16),
            pltpu.VMEM(new_keys.shape, BF16),
            pltpu.VMEM(new_keys.shape, BF16),
            pltpu.SemaphoreType.DMA((3,)),
        ],
        moved=queries.size * 4,
    )
    gap = call(
        gap_kernel, "gap", pltpu.VMEM((8, head_dim), F32), (payloads[0],), [VM], flops=GAP, moved=GAP,
    )
    payloads, gap = lax.optimization_barrier((payloads, gap))
    arrived = [payloads[0]] + [
        shift(payloads[step], "branch", step, nz) for step in range(nz - 1, 0, -1)
    ][::-1]
    chunk = math.gcd(positions * local, 1024)
    flat = (positions * local, head_dim)
    width = suffix * local
    slot_rows = (slots, width, head_dim)
    slot_keys, slot_values = suffix_keys.reshape(slot_rows), suffix_values.reshape(slot_rows)
    keys, values, token = call(
        functools.partial(split_kernel, local),
        "split",
        [pltpu.VMEM((local, positions, head_dim), BF16)] * 2 + [pltpu.VMEM((8, head_dim), F32)],
        (prefix_keys.reshape(flat), prefix_values.reshape(flat)),
        [VM] * 2,
        scratch=[pltpu.VMEM((chunk, head_dim), F32)],
        vmem=8 << 20,
        moved=prefix_keys.size * 8,
    )
    joined, fresh = call(
        functools.partial(join_kernel, nz, qrows),
        "join",
        [
            jax.ShapeDtypeStruct((nz, qrows, head_dim), BF16),
            jax.ShapeDtypeStruct((nz, padded - qrows, head_dim), BF16),
        ],
        (*arrived[::-1], gap, token),
        [VM] * (nz + 2),
        moved=nz * padded * head_dim * 4,
    )

    tail = ceil_to(3 * (rows // head_dim), 16)

    state = [jax.ShapeDtypeStruct((rows, head_dim), F32)] * 2

    def prefix(name, arrays, own=False):
        count = len(arrays)
        kernel = prefix_own_kernel if own else functools.partial(prefix_kernel, count)
        return call(
            functools.partial(kernel, local=local, qrows=qrows, scale=scale),
            name,
            state if own else [jax.ShapeDtypeStruct((rows + tail, head_dim), BF16)] * count,
            (*arrays, keys, values),
            [VM] * (count + 2),
            vmem=16 << 20,
            flops=4 * count * rows * positions * head_dim,
            moved=keys.size * 4,
        )

    far_steps = [(x, c) for x in range(1, nx) for c in range(nc)]
    near_steps = [(0, c) for c in range(1, nc)]
    arriving = {step: along_blk(joined, *step) for step in far_steps + near_steps}

    suffix_out, suffix_lse = call(
        functools.partial(suffix_kernel, nz, local, group, scale),
        "suffix",
        [jax.ShapeDtypeStruct((rows, head_dim), F32)] * 2,
        (
            joined, slot_branch, suffix_lengths, slot_keys, slot_values,
        ),
        [VM, SM, SM, VM, VM],
        scratch=[
            pltpu.VMEM((rows, head_dim), F32),
            pltpu.VMEM((slots * local * group, width), F32),
            pltpu.VMEM((slots * local * group, width), BF16),
        ],
        vmem=8 << 20,
        flops=4 * rows * width * head_dim,
        moved=suffix_keys.size * 4,
    )
    own_state = prefix("prefix_own", [joined], own=True)
    arriving, suffix_out, own_state = lax.optimization_barrier((arriving, suffix_out, own_state))

    def give_back(sent, steps):
        return [along_blk(x, back(step[0], nx), back(step[1], nc)) for x, step in zip(sent, steps)]

    received = []
    sent = []
    for i in range(0, len(far_steps), 2):
        steps = far_steps[i : i + 2]
        rows_of, sent = lax.optimization_barrier(([arriving[step] for step in steps], sent))
        sent = prefix("prefix_far", rows_of)
        received += give_back(sent, steps)
    sibling = []
    if near_steps:
        rows_of, sent = lax.optimization_barrier(([arriving[step] for step in near_steps], sent))
        sibling = give_back(prefix("prefix_near", rows_of), near_steps)
    near = call(
        functools.partial(near_kernel, len(sibling), local, group, scale),
        "near",
        state,
        (joined, fresh, suffix_out, suffix_lse, *own_state, *sibling),
        [VM] * (6 + len(sibling)),
        moved=rows * head_dim * 20,
    )
    pieces = call(
        functools.partial(final_kernel, len(received)),
        "final",
        [jax.ShapeDtypeStruct((qrows, head_dim), BF16)] * nz,
        (*near, *received),
        [VM] * (2 + len(received)),
        moved=rows * head_dim * 20,
    )
    landed = [pieces[0]] + [
        shift(pieces[step], "branch", back(step, nz), nz) for step in range(nz - 1, 0, -1)
    ][::-1]
    out = call(
        functools.partial(unpack_kernel, nz, local, group),
        "unpack",
        jax.ShapeDtypeStruct((nb, nz, heads // nz, head_dim), BF16),
        landed[::-1],
        [VM] * nz,
        moved=queries.size * 4,
    )
    return out.reshape(nb, heads, head_dim)


def solution(mesh):
    lanes = P(("groups", "blk", "branch"), None, None)
    return jax.shard_map(
        functools.partial(per_device, mesh.shape["branch"], mesh.shape["blk"]),
        mesh=mesh,
        in_specs=(
            lanes,
            lanes,
            lanes,
            P(("groups", "blk"), "branch", None),
            P(("groups", "blk"), "branch", None),
            P(("groups", "blk"), None, "branch", None),
            P(("groups", "blk"), None, "branch", None),
            P("groups"),
            P("groups"),
        ),
        out_specs=lanes,
        check_vma=False,
    )
```

```python
import functools
import math

import jax
import jax.numpy as jnp
from jax import lax
from jax.experimental import pallas as pl
from jax.experimental.pallas import tpu as pltpu
from jax.sharding import PartitionSpec as P

NEG = -1e30
GAP = 1 << 36
SUF_F = 0
SUF_M = 0
LOG2E = 1.4426950408889634
F32 = jnp.float32
BF16 = jnp.bfloat16
VM = pl.BlockSpec(memory_space=pltpu.VMEM)
SM = pl.BlockSpec(memory_space=pltpu.SMEM)
HBM = pl.BlockSpec(memory_space=pltpu.HBM)
NT = (((1,), (1,)), ((), ()))


def ceil_to(value, unit):
    return -(-value // unit) * unit


def partner(index, step, count):
    if count & (count - 1) == 0:
        return index ^ step
    return (index + step) % count


def back(step, count):
    return step if count & (count - 1) == 0 else (count - step) % count


def step_to(me, other, count):
    if count & (count - 1) == 0:
        return me ^ other
    return lax.rem(me - other + count, count)


def in_hbm(x):
    return pltpu.with_memory_space_constraint(x, pltpu.HBM)


def call(kernel, name, out_shape, inputs, in_specs, scratch=(), vmem=16 << 20, flops=0, moved=0, out_specs=None):
    many = isinstance(out_shape, (list, tuple))
    return pl.pallas_call(
        kernel,
        name=name,
        out_shape=out_shape,
        in_specs=in_specs,
        out_specs=out_specs if out_specs is not None else ([VM] * len(out_shape) if many else VM),
        scratch_shapes=list(scratch),
        compiler_params=pltpu.CompilerParams(vmem_limit_bytes=vmem),
        cost_estimate=pl.CostEstimate(flops=flops, bytes_accessed=moved, transcendentals=0),
    )(*inputs)


def pack_kernel(nz, local, group, pad, q_hbm, k_hbm, v_hbm, *refs):
    out_refs, (q_ref, k_ref, v_ref, sems) = refs[:nz], refs[nz:]
    copies = [
        pltpu.make_async_copy(src, dst, sems.at[i])
        for i, (src, dst) in enumerate(((q_hbm, q_ref), (k_hbm, k_ref), (v_hbm, v_ref)))
    ]
    for copy in copies:
        copy.start()
    for copy in copies:
        copy.wait()
    me = lax.axis_index("branch")
    nb = q_ref.shape[0]
    head_dim = q_ref.shape[-1]
    new_k = k_ref[...].astype(F32)
    new_v = v_ref[...].astype(F32)
    for step in range(nz):
        peer = partner(me, step, nz)
        q = q_ref[:, peer].astype(F32)
        parts = [
            q[:, kl * group : (kl + 1) * group].reshape(nb * group, head_dim) for kl in range(local)
        ]
        rows_k, rows_v = new_k[:, :local], new_v[:, :local]
        for z in range(1, nz):
            here = peer == z
            rows_k = jnp.where(here, new_k[:, z * local : (z + 1) * local], rows_k)
            rows_v = jnp.where(here, new_v[:, z * local : (z + 1) * local], rows_v)
        for rows in (rows_k, rows_v):
            for kl in range(local):
                parts += [rows[b, kl : kl + 1] for b in range(nb)]
        if pad:
            parts.append(jnp.zeros((pad, head_dim), F32))
        out_refs[step][...] = jnp.concatenate(parts, axis=0).astype(BF16)


def join_kernel(nz, qrows, *refs):
    q_ref, tail_ref = refs[-2:]
    for step in range(nz):
        q_ref[step] = refs[nz - 1 - step][:qrows]
        tail_ref[step] = refs[nz - 1 - step][qrows:]


def gap_kernel(after, token):
    token[...] = jnp.zeros(token.shape, token.dtype)


def split_kernel(local, pk, pv, pko, pvo, token, wide):
    token[...] = jnp.zeros(token.shape, token.dtype)
    chunk = wide.shape[0]
    rows = chunk // local
    for src, dst in ((pk, pko), (pv, pvo)):
        for at in range(src.shape[0] // chunk):
            if local == 1:
                dst[0, at * rows : (at + 1) * rows] = src[at * chunk : (at + 1) * chunk]
                continue
            wide[...] = src[at * chunk : (at + 1) * chunk].astype(F32)
            for kl in range(local):
                dst[kl, at * rows : (at + 1) * rows] = wide[pl.ds(kl, rows, stride=local)].astype(BF16)


def suffix_kernel(
    nz, local, group, scale, joined_ref, slot_ref, len_ref, keys, values, out_ref, lse_ref,
    qwide, scores, probs
):
    slots, width, head_dim = keys.shape
    block = lax.axis_index("blk")
    me = lax.axis_index("branch")
    nb = slots // nz
    qrows = local * nb * group
    for step in range(nz):
        qwide[step * qrows : (step + 1) * qrows] = joined_ref[step, :qrows].astype(F32)
    heads = local * group
    column = lax.broadcasted_iota(jnp.int32, (heads, width), 1)
    row = lax.broadcasted_iota(jnp.int32, (heads, width), 0)
    own_head = lax.rem(column, local) == row // group

    def places(c):
        branch = slot_ref[block * slots + c]
        length = len_ref[branch]
        branch = branch - block * slots
        step = step_to(me, branch // nb, nz)
        at = step * qrows + lax.rem(branch, nb) * group
        return [pl.multiple_of(at + kl * nb * group, 8) for kl in range(local)], length

    for c in range(slots):
        at, length = places(c)
        q = jnp.concatenate([qwide[pl.ds(a, group)] for a in at], axis=0).astype(BF16)
        s = lax.dot_general(q, keys[c], NT, preferred_element_type=F32)
        scores[c * heads : (c + 1) * heads] = jnp.where(
            own_head & (column < length * local), s, NEG
        )
    s = scores[...]
    top = jnp.max(s, axis=-1, keepdims=True)
    weights = jnp.exp2((s - top) * (scale * LOG2E))
    total = jnp.sum(weights, axis=-1, keepdims=True)
    probs[...] = weights.astype(BF16)
    lse = top * scale + jnp.log(total)
    inverse = 1.0 / total
    for c in range(slots):
        at, _ = places(c)
        o = jnp.dot(probs[c * heads : (c + 1) * heads], values[c], preferred_element_type=F32)
        o = o * inverse[c * heads : (c + 1) * heads]
        for kl in range(local):
            lo, hi = kl * group, (kl + 1) * group
            out_ref[pl.ds(at[kl], group)] = o[lo:hi]
            lse_ref[pl.ds(at[kl], group)] = jnp.broadcast_to(
                lse[c * heads + lo : c * heads + hi], (group, head_dim)
            )


def column_to_rows(column, lanes):
    count = column.shape[0] // lanes
    eye = lax.broadcasted_iota(jnp.int32, (lanes, lanes), 0) == lax.broadcasted_iota(
        jnp.int32, (lanes, lanes), 1
    )
    rows = [
        jnp.sum(jnp.where(eye, column[i * lanes : (i + 1) * lanes], 0.0), axis=0, keepdims=True)
        for i in range(count)
    ]
    return jnp.concatenate(rows, axis=0)


def rows_to_column(rows):
    lanes = rows.shape[1]
    eye = lax.broadcasted_iota(jnp.int32, (lanes, lanes), 0) == lax.broadcasted_iota(
        jnp.int32, (lanes, lanes), 1
    )
    parts = [
        jnp.sum(jnp.where(eye, rows[i : i + 1], 0.0), axis=1, keepdims=True)
        for i in range(rows.shape[0])
    ]
    return jnp.concatenate(parts, axis=0)


def encode(out, lse):
    lanes = out.shape[1]
    rows = column_to_rows(lse, lanes)
    high = rows.astype(BF16).astype(F32)
    middle = (rows - high).astype(BF16).astype(F32)
    low = rows - high - middle
    tail = [high, middle, low]
    used = 3 * rows.shape[0]
    tail.append(jnp.zeros((ceil_to(used, 16) - used, lanes), F32))
    return jnp.concatenate([out] + tail, axis=0).astype(BF16)


def decode(payload, count):
    wide = payload.astype(F32)
    lanes = wide.shape[1]
    n = count // lanes
    rows = wide[count : count + n] + wide[count + n : count + 2 * n] + wide[count + 2 * n : count + 3 * n]
    return wide[:count], rows_to_column(rows)


def merge(parts):
    top = parts[0][1]
    for _, lse in parts[1:]:
        top = jnp.maximum(top, lse)
    weights = [jnp.exp2((lse - top) * LOG2E) for _, lse in parts]
    total = sum(weights[1:], weights[0])
    out = parts[0][0] * weights[0]
    for (o, _), w in zip(parts[1:], weights[1:]):
        out = out + o * w
    return out * (1.0 / total), top + jnp.log(total)


def prefix_partial(q_refs, k_ref, v_ref, local, qrows, scale):
    part = qrows // local
    steps = q_refs[0].shape[0]
    outs, lses = [], []
    for kl in range(local):
        q = jnp.concatenate(
            [ref[z, kl * part : (kl + 1) * part] for ref in q_refs for z in range(steps)], axis=0
        )
        s = lax.dot_general(q, k_ref[kl], NT, preferred_element_type=F32)
        top = jnp.max(s, axis=-1, keepdims=True)
        weights = jnp.exp2((s - top) * (scale * LOG2E))
        total = jnp.sum(weights, axis=-1, keepdims=True)
        o = jnp.dot(weights.astype(BF16), v_ref[kl], preferred_element_type=F32)
        outs.append(o * (1.0 / total))
        lses.append(top * scale + jnp.log(total))
    results = []
    for i in range(len(q_refs)):
        pieces = [(i * steps + z) * part for z in range(steps)]
        results.append(
            tuple(
                jnp.concatenate([a[p : p + part] for p in pieces for a in arrays], axis=0)
                for arrays in (outs, lses)
            )
        )
    return results


def prefix_kernel(count, *refs, local, qrows, scale):
    q_refs, (k_ref, v_ref), outs = refs[:count], refs[count : count + 2], refs[count + 2 :]
    for ref, (o, lse) in zip(outs, prefix_partial(q_refs, k_ref, v_ref, local, qrows, scale)):
        ref[...] = encode(o, lse)


def prefix_own_kernel(q_ref, k_ref, v_ref, o_ref, lse_ref, *, local, qrows, scale):
    ((o, lse),) = prefix_partial([q_ref], k_ref, v_ref, local, qrows, scale)
    o_ref[...] = o
    lse_ref[...] = jnp.broadcast_to(lse, o.shape)


def near_kernel(count, local, group, scale, q_ref, fresh_ref, so_ref, sl_ref, po_ref, pl_ref, *refs):
    others, (out_ref, lse_ref) = refs[:count], refs[count:]
    rows, head_dim = po_ref.shape
    nz, qrows = q_ref.shape[:2]
    part = qrows // group
    own_score, own_value = [], []
    for step in range(nz):
        q = q_ref[step].astype(F32)
        tail = fresh_ref[step].astype(F32)
        k, v = (
            jnp.concatenate(
                [jnp.broadcast_to(tail[i : i + 1], (group, head_dim)) for i in range(at, at + part)],
                axis=0,
            )
            for at in (0, part)
        )
        own_score.append(jnp.sum(q * k, axis=1, keepdims=True) * scale)
        own_value.append(v)
    parts = [
        (jnp.concatenate(own_value, axis=0), jnp.concatenate(own_score, axis=0)),
        (so_ref[...], sl_ref[:, :1]),
        (po_ref[...], pl_ref[:, :1]),
    ]
    parts += [decode(ref[...], rows) for ref in others]
    out, lse = merge(parts)
    out_ref[...] = out
    lse_ref[...] = jnp.broadcast_to(lse, out.shape)


def final_kernel(count, near_ref, lse_ref, *refs):
    others, outs = refs[:count], refs[count:]
    parts = [(near_ref[...], lse_ref[:, :1])]
    parts += [decode(ref[...], near_ref.shape[0]) for ref in others]
    out, _ = merge(parts)
    qrows = outs[0].shape[0]
    for step, ref in enumerate(outs):
        ref[...] = out[step * qrows : (step + 1) * qrows].astype(BF16)


def unpack_kernel(nz, local, group, *refs):
    pieces, out_ref = refs[:nz], refs[nz]
    me = lax.axis_index("branch")
    nb = out_ref.shape[0]
    for step in range(nz):
        peer = partner(me, step, nz)
        wide = pieces[nz - 1 - step][...].astype(F32)
        for b in range(nb):
            rows = [wide[(kl * nb + b) * group : (kl * nb + b + 1) * group] for kl in range(local)]
            out_ref[b, peer] = jnp.concatenate(rows, axis=0).astype(BF16)


def per_device(
    nz, nblk, queries, new_keys, fresh_token_values, prefix_keys, prefix_values, suffix_keys,
    suffix_values, suffix_lengths, slot_branch
):
    nb, heads, head_dim = queries.shape
    positions, local = prefix_keys.shape[:2]
    group = heads // new_keys.shape[1]
    slots, suffix = suffix_keys.shape[:2]
    scale = 1.0 / math.sqrt(head_dim)
    qrows = local * nb * group
    used = qrows + 2 * nb * local
    padded = ceil_to(used, 16)
    rows = nz * qrows
    nc = 2 if nblk % 2 == 0 else 1
    nx = nblk // nc

    def shift(x, axis, step, count):
        return lax.ppermute(x, axis, [(i, partner(i, step, count)) for i in range(count)])

    def along_blk(x, step_x, step_c):
        return lax.ppermute(
            x,
            "blk",
            [
                (i, partner(i // nc, step_x, nx) * nc + partner(i % nc, step_c, nc))
                for i in range(nblk)
            ],
        )

    payloads = call(
        functools.partial(pack_kernel, nz, local, group, padded - used),
        "pack",
        [pltpu.VMEM((padded, head_dim), BF16)] * nz,
        (
            in_hbm(queries.reshape(nb, nz, heads // nz, head_dim)),
            in_hbm(new_keys), in_hbm(fresh_token_values),
        ),
        [HBM] * 3,
        scratch=[
            pltpu.VMEM((nb, nz, heads // nz, head_dim), BF16),
            pltpu.VMEM(new_keys.shape, BF16),
            pltpu.VMEM(new_keys.shape, BF16),
            pltpu.SemaphoreType.DMA((3,)),
        ],
        moved=queries.size * 4,
    )
    gap = call(
        gap_kernel, "gap", pltpu.VMEM((8, head_dim), F32), (payloads[0],), [VM], flops=GAP, moved=GAP,
    )
    payloads, gap = lax.optimization_barrier((payloads, gap))
    arrived = [payloads[0]] + [
        shift(payloads[step], "branch", step, nz) for step in range(nz - 1, 0, -1)
    ][::-1]
    chunk = math.gcd(positions * local, 1024)
    flat = (positions * local, head_dim)
    width = suffix * local
    slot_rows = (slots, width, head_dim)
    slot_keys, slot_values = suffix_keys.reshape(slot_rows), suffix_values.reshape(slot_rows)
    keys, values, token = call(
        functools.partial(split_kernel, local),
        "split",
        [pltpu.VMEM((local, positions, head_dim), BF16)] * 2 + [pltpu.VMEM((8, head_dim), F32)],
        (prefix_keys.reshape(flat), prefix_values.reshape(flat)),
        [VM] * 2,
        scratch=[pltpu.VMEM((chunk, head_dim), F32)],
        vmem=8 << 20,
        moved=prefix_keys.size * 8,
    )
    joined, fresh = call(
        functools.partial(join_kernel, nz, qrows),
        "join",
        [
            jax.ShapeDtypeStruct((nz, qrows, head_dim), BF16),
            jax.ShapeDtypeStruct((nz, padded - qrows, head_dim), BF16),
        ],
        (*arrived[::-1], gap, token),
        [VM] * (nz + 2),
        moved=nz * padded * head_dim * 4,
    )

    tail = ceil_to(3 * (rows // head_dim), 16)

    state = [jax.ShapeDtypeStruct((rows, head_dim), F32)] * 2

    def prefix(name, arrays, own=False):
        count = len(arrays)
        kernel = prefix_own_kernel if own else functools.partial(prefix_kernel, count)
        return call(
            functools.partial(kernel, local=local, qrows=qrows, scale=scale),
            name,
            state if own else [jax.ShapeDtypeStruct((rows + tail, head_dim), BF16)] * count,
            (*arrays, keys, values),
            [VM] * (count + 2),
            vmem=16 << 20,
            flops=4 * count * rows * positions * head_dim,
            moved=keys.size * 4,
        )

    far_steps = [(x, c) for x in range(1, nx) for c in range(nc)]
    near_steps = [(0, c) for c in range(1, nc)]
    arriving = {step: along_blk(joined, *step) for step in far_steps + near_steps}

    own_state = prefix("prefix_own", [joined], own=True)
    def give_back(x, step):
        return along_blk(x, back(step[0], nx), back(step[1], nc))

    steps = far_steps[::-1] + near_steps
    groups = [steps[:1]] + [steps[i : i + 2] for i in range(1, len(steps), 2)]
    received = {}
    sent = list(own_state)
    for group_of in [g for g in groups if g]:
        rows_of, sent = lax.optimization_barrier(([arriving[step] for step in group_of], sent))
        if group_of is groups[0]:
            own_state = sent
        sent = prefix("prefix_far", rows_of)
        for x, step in zip(sent, group_of):
            received[step] = give_back(x, step)
    sent, slot_keys = lax.optimization_barrier((sent, slot_keys))
    suffix_out, suffix_lse = call(
        functools.partial(suffix_kernel, nz, local, group, scale),
        "suffix",
        state,
        (joined, slot_branch, suffix_lengths, slot_keys, slot_values),
        [VM, SM, SM, VM, VM],
        scratch=[
            pltpu.VMEM((rows, head_dim), F32),
            pltpu.VMEM((slots * local * group, width), F32),
            pltpu.VMEM((slots * local * group, width), BF16),
        ],
        vmem=8 << 20,
        flops=SUF_F,
        moved=SUF_M,
    )
    last = [received.pop(step) for step in groups[-1]] if steps else []
    others = list(received.values())
    near = call(
        functools.partial(near_kernel, len(others), local, group, scale),
        "near",
        state,
        (joined, fresh, suffix_out, suffix_lse, *own_state, *others),
        [VM] * (6 + len(others)),
        moved=rows * head_dim * 20,
    )
    received = last
    pieces = call(
        functools.partial(final_kernel, len(received)),
        "final",
        [jax.ShapeDtypeStruct((qrows, head_dim), BF16)] * nz,
        (*near, *received),
        [VM] * (2 + len(received)),
        moved=rows * head_dim * 20,
    )
    landed = [pieces[0]] + [
        shift(pieces[step], "branch", back(step, nz), nz) for step in range(nz - 1, 0, -1)
    ][::-1]
    out = call(
        functools.partial(unpack_kernel, nz, local, group),
        "unpack",
        jax.ShapeDtypeStruct((nb, nz, heads // nz, head_dim), BF16),
        landed[::-1],
        [VM] * nz,
        moved=queries.size * 4,
    )
    return out.reshape(nb, heads, head_dim)


def solution(mesh):
    lanes = P(("groups", "blk", "branch"), None, None)
    return jax.shard_map(
        functools.partial(per_device, mesh.shape["branch"], mesh.shape["blk"]),
        mesh=mesh,
        in_specs=(
            lanes,
            lanes,
            lanes,
            P(("groups", "blk"), "branch", None),
            P(("groups", "blk"), "branch", None),
            P(("groups", "blk"), None, "branch", None),
            P(("groups", "blk"), None, "branch", None),
            P("groups"),
            P("groups"),
        ),
        out_specs=lanes,
        check_vma=False,
    )
```

```python
import functools
import math

import jax
import jax.numpy as jnp
from jax import lax
from jax.experimental import pallas as pl
from jax.experimental.pallas import tpu as pltpu
from jax.sharding import PartitionSpec as P

NEG = -1e30
GAP = 1 << 36
LOG2E = 1.4426950408889634
F32 = jnp.float32
BF16 = jnp.bfloat16
VM = pl.BlockSpec(memory_space=pltpu.VMEM)
SM = pl.BlockSpec(memory_space=pltpu.SMEM)
HBM = pl.BlockSpec(memory_space=pltpu.HBM)
NT = (((1,), (1,)), ((), ()))


def ceil_to(value, unit):
    return -(-value // unit) * unit


def partner(index, step, count):
    if count & (count - 1) == 0:
        return index ^ step
    return (index + step) % count


def back(step, count):
    return step if count & (count - 1) == 0 else (count - step) % count


def step_to(me, other, count):
    if count & (count - 1) == 0:
        return me ^ other
    return lax.rem(me - other + count, count)


def in_hbm(x):
    return pltpu.with_memory_space_constraint(x, pltpu.HBM)


def call(kernel, name, out_shape, inputs, in_specs, scratch=(), vmem=16 << 20, flops=0, moved=0, out_specs=None):
    many = isinstance(out_shape, (list, tuple))
    return pl.pallas_call(
        kernel,
        name=name,
        out_shape=out_shape,
        in_specs=in_specs,
        out_specs=out_specs if out_specs is not None else ([VM] * len(out_shape) if many else VM),
        scratch_shapes=list(scratch),
        compiler_params=pltpu.CompilerParams(vmem_limit_bytes=vmem),
        cost_estimate=pl.CostEstimate(flops=flops, bytes_accessed=moved, transcendentals=0),
    )(*inputs)


def pack_kernel(nz, local, group, pad, q_hbm, k_hbm, v_hbm, *refs):
    out_refs, (q_ref, k_ref, v_ref, sems) = refs[:nz], refs[nz:]
    copies = [
        pltpu.make_async_copy(src, dst, sems.at[i])
        for i, (src, dst) in enumerate(((q_hbm, q_ref), (k_hbm, k_ref), (v_hbm, v_ref)))
    ]
    for copy in copies:
        copy.start()
    for copy in copies:
        copy.wait()
    me = lax.axis_index("branch")
    nb = q_ref.shape[0]
    head_dim = q_ref.shape[-1]
    new_k = k_ref[...].astype(F32)
    new_v = v_ref[...].astype(F32)
    for step in range(nz):
        peer = partner(me, step, nz)
        q = q_ref[:, peer].astype(F32)
        parts = [
            q[:, kl * group : (kl + 1) * group].reshape(nb * group, head_dim) for kl in range(local)
        ]
        rows_k, rows_v = new_k[:, :local], new_v[:, :local]
        for z in range(1, nz):
            here = peer == z
            rows_k = jnp.where(here, new_k[:, z * local : (z + 1) * local], rows_k)
            rows_v = jnp.where(here, new_v[:, z * local : (z + 1) * local], rows_v)
        for rows in (rows_k, rows_v):
            for kl in range(local):
                parts += [rows[b, kl : kl + 1] for b in range(nb)]
        if pad:
            parts.append(jnp.zeros((pad, head_dim), F32))
        out_refs[step][...] = jnp.concatenate(parts, axis=0).astype(BF16)


def join_kernel(nz, qrows, *refs):
    q_ref, tail_ref = refs[-2:]
    for step in range(nz):
        q_ref[step] = refs[nz - 1 - step][:qrows]
        tail_ref[step] = refs[nz - 1 - step][qrows:]


def gap_kernel(after, token):
    token[...] = jnp.zeros(token.shape, token.dtype)


def split_kernel(local, pk, pv, pko, pvo, token, wide):
    token[...] = jnp.zeros(token.shape, token.dtype)
    chunk = wide.shape[0]
    rows = chunk // local
    for src, dst in ((pk, pko), (pv, pvo)):
        for at in range(src.shape[0] // chunk):
            wide[...] = src[at * chunk : (at + 1) * chunk].astype(F32)
            for kl in range(local):
                head = wide[pl.ds(kl, rows, stride=local)] if local > 1 else wide[...]
                if dst is pvo:
                    dst[kl, :, at * rows : (at + 1) * rows] = head.T.astype(BF16)
                else:
                    dst[kl, at * rows : (at + 1) * rows] = head.astype(BF16)


def places(c, slots, nz, local, group, slot_ref, len_ref):
    first = lax.axis_index("blk") * slots
    branch = slot_ref[first + c]
    length = len_ref[branch]
    branch = branch - first
    nb = slots // nz
    step = step_to(lax.axis_index("branch"), branch // nb, nz)
    at = step * (nb * group) + lax.rem(branch, nb) * group
    return [pl.multiple_of(at + kl * (slots * group), 8) for kl in range(local)], length


def suffix_scores_kernel(nz, local, group, scale, q_ref, slot_ref, len_ref, keys, probs, lse_ref, inv_ref, qwide, scores):
    slots, width, head_dim = keys.shape
    part = slots // nz * group
    for step in range(nz):
        for kl in range(local):
            at = kl * nz * part + step * part
            qwide[at : at + part] = q_ref[step, kl * part : (kl + 1) * part].astype(F32)
    heads = local * group
    column = lax.broadcasted_iota(jnp.int32, (heads, width), 1)
    row = lax.broadcasted_iota(jnp.int32, (heads, width), 0)
    own_head = lax.rem(column, local) == row // group
    for c in range(slots):
        at, length = places(c, slots, nz, local, group, slot_ref, len_ref)
        q = jnp.concatenate([qwide[pl.ds(a, group)] for a in at], axis=0).astype(BF16)
        s = lax.dot_general(q, keys[c], NT, preferred_element_type=F32)
        scores[c * heads : (c + 1) * heads] = jnp.where(
            own_head & (column < length * local), s, NEG
        )
    s = scores[...]
    top = jnp.max(s, axis=-1, keepdims=True)
    weights = jnp.exp2((s - top) * (scale * LOG2E))
    total = jnp.sum(weights, axis=-1, keepdims=True)
    probs[...] = weights.astype(BF16)
    lse_ref[...] = jnp.broadcast_to(top * scale + jnp.log(total), lse_ref.shape)
    inv_ref[...] = jnp.broadcast_to(1.0 / total, inv_ref.shape)


def suffix_values_kernel(nz, local, group, slot_ref, len_ref, values, probs, slot_lse, slot_inv, out_ref, lse_ref):
    slots = values.shape[0]
    heads = local * group
    for c in range(slots):
        at, _ = places(c, slots, nz, local, group, slot_ref, len_ref)
        rows = slice(c * heads, (c + 1) * heads)
        o = jnp.dot(probs[rows], values[c], preferred_element_type=F32) * slot_inv[rows]
        lse = slot_lse[rows]
        for kl in range(local):
            lo, hi = kl * group, (kl + 1) * group
            out_ref[pl.ds(at[kl], group)] = o[lo:hi]
            lse_ref[pl.ds(at[kl], group)] = lse[lo:hi]


def encode(outs, lses):
    rows = jnp.concatenate(lses, axis=0)
    high = rows.astype(BF16).astype(F32)
    middle = (rows - high).astype(BF16).astype(F32)
    low = rows - high - middle
    used = 3 * rows.shape[0]
    pad = jnp.zeros((ceil_to(used, 16) - used, rows.shape[1]), F32)
    return jnp.concatenate([*outs, high, middle, low, pad], axis=0).astype(BF16)


def decode(payload, local):
    wide = payload.astype(F32)
    count = wide.shape[0] - ceil_to(3 * local, 16)
    size = count // local
    parts = []
    for kl in range(local):
        high, middle, low = (wide[count + i * local + kl :][:1] for i in range(3))
        parts.append((wide[kl * size : (kl + 1) * size], high + middle + low))
    return parts


def merge(parts):
    top = parts[0][1]
    for _, lse in parts[1:]:
        top = jnp.maximum(top, lse)
    weights = [jnp.exp2((lse - top) * LOG2E) for _, lse in parts]
    total = sum(weights[1:], weights[0])
    inverse = 1.0 / total
    out = parts[0][0] * (weights[0] * inverse)
    for (o, _), w in zip(parts[1:], weights[1:]):
        out = out + o * (w * inverse)
    return out, top + jnp.log(total)


def prefix_kernel(count, own, local, scale, *refs):
    q_refs, (k_ref, v_ref), outs = refs[:count], refs[count : count + 2], refs[count + 2 :]
    steps, qrows = q_refs[0].shape[:2]
    part = qrows // local
    columns = steps * part
    heads = []
    for kl in range(local):
        q = jnp.concatenate(
            [ref[z, kl * part : (kl + 1) * part] for ref in q_refs for z in range(steps)], axis=0
        )
        s = lax.dot_general(k_ref[kl], q, NT, preferred_element_type=F32)
        top = jnp.max(s, axis=0, keepdims=True)
        weights = jnp.exp2((s - top) * (scale * LOG2E))
        total = jnp.sum(weights, axis=0, keepdims=True)
        o = jnp.dot(v_ref[kl], weights.astype(BF16), preferred_element_type=F32)
        heads.append((o * (1.0 / total), top * scale + jnp.log(total)))
    for i in range(count):
        at = slice(i * columns, (i + 1) * columns)
        os, lses = [o[:, at] for o, _ in heads], [lse[:, at] for _, lse in heads]
        if own and i == count - 1:
            outs[i][...] = jnp.concatenate(os, axis=0)
            outs[i + 1][:local] = jnp.concatenate(lses, axis=0)
        else:
            outs[i][...] = encode(os, lses)


def near_kernel(count, local, group, scale, q_ref, fresh_ref, so_ref, sl_ref, po_ref, pl_ref, *refs):
    others, (out_ref, lse_ref) = refs[:count], refs[count:]
    nz, qrows = q_ref.shape[:2]
    part = qrows // local
    nb = part // group
    columns = nz * part
    head_dim = so_ref.shape[1]
    decoded = [decode(ref[...], local) for ref in others]
    for kl in range(local):
        scores, news = [], []
        for step in range(nz):
            q = q_ref[step, kl * part : (kl + 1) * part].astype(F32)
            tail = fresh_ref[step].astype(F32)
            k, v = (
                jnp.concatenate(
                    [
                        jnp.broadcast_to(tail[i : i + 1], (group, head_dim))
                        for i in range(at + kl * nb, at + (kl + 1) * nb)
                    ],
                    axis=0,
                )
                for at in (0, nb * local)
            )
            scores.append(jnp.sum(q * k, axis=1, keepdims=True) * scale)
            news.append(v)
        rows = slice(kl * columns, (kl + 1) * columns)
        out, lse = merge(
            [
                (jnp.concatenate(news, axis=0), jnp.concatenate(scores, axis=0)),
                (so_ref[rows], sl_ref[rows]),
            ]
        )
        at = slice(kl * head_dim, (kl + 1) * head_dim)
        parts = [(out.T, lse.T[:1]), (po_ref[at], pl_ref[kl : kl + 1])]
        out, lse = merge(parts + [d[kl] for d in decoded])
        out_ref[at] = out
        lse_ref[kl : kl + 1] = lse


def final_kernel(count, local, near_ref, lse_ref, *refs):
    others, outs = refs[:count], refs[count:]
    head_dim = near_ref.shape[0] // local
    part = outs[0].shape[0] // local
    decoded = [decode(ref[...], local) for ref in others]
    for kl in range(local):
        at = slice(kl * head_dim, (kl + 1) * head_dim)
        out, _ = merge([(near_ref[at], lse_ref[kl : kl + 1])] + [d[kl] for d in decoded])
        out = out.T
        for step, ref in enumerate(outs):
            ref[kl * part : (kl + 1) * part] = out[step * part : (step + 1) * part].astype(BF16)


def unpack_kernel(nz, local, group, *refs):
    pieces, out_ref = refs[:nz], refs[nz]
    me = lax.axis_index("branch")
    nb = out_ref.shape[0]
    for step in range(nz):
        peer = partner(me, step, nz)
        wide = pieces[nz - 1 - step][...].astype(F32)
        for b in range(nb):
            rows = [wide[(kl * nb + b) * group : (kl * nb + b + 1) * group] for kl in range(local)]
            out_ref[b, peer] = jnp.concatenate(rows, axis=0).astype(BF16)


def per_device(
    nz, nblk, queries, new_keys, fresh_token_values, prefix_keys, prefix_values, suffix_keys,
    suffix_values, suffix_lengths, slot_branch
):
    nb, heads, head_dim = queries.shape
    positions, local = prefix_keys.shape[:2]
    group = heads // new_keys.shape[1]
    slots, suffix = suffix_keys.shape[:2]
    scale = 1.0 / math.sqrt(head_dim)
    qrows = local * nb * group
    used = qrows + 2 * nb * local
    padded = ceil_to(used, 16)
    rows = nz * qrows
    nc = 2 if nblk % 2 == 0 else 1
    nx = nblk // nc

    def shift(x, axis, step, count):
        return lax.ppermute(x, axis, [(i, partner(i, step, count)) for i in range(count)])

    def along_blk(x, step_x, step_c):
        return lax.ppermute(
            x,
            "blk",
            [
                (i, partner(i // nc, step_x, nx) * nc + partner(i % nc, step_c, nc))
                for i in range(nblk)
            ],
        )

    payloads = call(
        functools.partial(pack_kernel, nz, local, group, padded - used),
        "pack",
        [pltpu.VMEM((padded, head_dim), BF16)] * nz,
        (
            in_hbm(queries.reshape(nb, nz, heads // nz, head_dim)),
            in_hbm(new_keys), in_hbm(fresh_token_values),
        ),
        [HBM] * 3,
        scratch=[
            pltpu.VMEM((nb, nz, heads // nz, head_dim), BF16),
            pltpu.VMEM(new_keys.shape, BF16),
            pltpu.VMEM(new_keys.shape, BF16),
            pltpu.SemaphoreType.DMA((3,)),
        ],
        moved=queries.size * 4,
    )
    gap = call(
        gap_kernel, "gap", pltpu.VMEM((8, head_dim), F32), (payloads[0],), [VM], flops=GAP, moved=GAP,
    )
    payloads, gap = lax.optimization_barrier((payloads, gap))
    arrived = [payloads[0]] + [
        shift(payloads[step], "branch", step, nz) for step in range(nz - 1, 0, -1)
    ][::-1]
    chunk = math.gcd(positions * local, 1024)
    flat = (positions * local, head_dim)
    width = suffix * local
    slot_rows = (slots, width, head_dim)
    slot_keys, slot_values = suffix_keys.reshape(slot_rows), suffix_values.reshape(slot_rows)
    keys, values, token = call(
        functools.partial(split_kernel, local),
        "split",
        [
            pltpu.VMEM((local, positions, head_dim), BF16),
            pltpu.VMEM((local, head_dim, positions), BF16),
            pltpu.VMEM((8, head_dim), F32),
        ],
        (prefix_keys.reshape(flat), prefix_values.reshape(flat)),
        [VM] * 2,
        scratch=[pltpu.VMEM((chunk, head_dim), F32)],
        vmem=8 << 20,
        moved=prefix_keys.size * 8,
    )
    joined, fresh = call(
        functools.partial(join_kernel, nz, qrows),
        "join",
        [
            jax.ShapeDtypeStruct((nz, qrows, head_dim), BF16),
            jax.ShapeDtypeStruct((nz, padded - qrows, head_dim), BF16),
        ],
        (*arrived[::-1], gap, token),
        [VM] * (nz + 2),
        moved=nz * padded * head_dim * 4,
    )

    columns = rows // local
    state = [
        jax.ShapeDtypeStruct((local * head_dim, columns), F32),
        jax.ShapeDtypeStruct((ceil_to(local, 8), columns), F32),
    ]
    payload = jax.ShapeDtypeStruct((local * head_dim + ceil_to(3 * local, 16), columns), BF16)

    def prefix(name, arrays, own=False):
        count = len(arrays)
        return call(
            functools.partial(prefix_kernel, count, own, local, scale),
            name,
            [payload] * (count - own) + (state if own else []),
            (*arrays, keys, values),
            [VM] * (count + 2),
            vmem=16 << 20,
            flops=4 * count * rows * positions * head_dim,
            moved=keys.size * 4,
        )

    far_steps = [(x, c) for x in range(1, nx) for c in range(nc)]
    near_steps = [(0, c) for c in range(1, nc)]
    arriving = {step: along_blk(joined, *step) for step in far_steps + near_steps}

    heads_here = local * group
    flat_state = [jax.ShapeDtypeStruct((rows, head_dim), F32)] * 2
    probs, slot_lse, slot_inv = call(
        functools.partial(suffix_scores_kernel, nz, local, group, scale),
        "suffix_scores",
        [jax.ShapeDtypeStruct((slots * heads_here, width), BF16)] + flat_state,
        (joined, slot_branch, suffix_lengths, slot_keys),
        [VM, SM, SM, VM],
        scratch=[
            pltpu.VMEM((rows, head_dim), F32),
            pltpu.VMEM((slots * heads_here, width), F32),
        ],
        vmem=8 << 20,
        flops=2 * rows * width * head_dim,
        moved=suffix_keys.size * 2,
    )

    def give_back(x, step):
        return along_blk(x, back(step[0], nx), back(step[1], nc))

    steps = far_steps[::-1] + near_steps
    groups = [steps[:1]] + [steps[i : i + 2] for i in range(1, len(steps), 2)]
    received = {}
    sent = [probs]
    for i, group_of in enumerate(g for g in groups):
        rows_of, sent = lax.optimization_barrier(([arriving[step] for step in group_of], sent))
        if i == 0:
            (probs,) = sent
            *sent, own_out, own_lse = prefix("prefix_own", [*rows_of, joined], own=True)
        else:
            sent = prefix("prefix_far", rows_of)
        for x, step in zip(sent, group_of):
            received[step] = give_back(x, step)
    sent, probs = lax.optimization_barrier((sent, probs))
    suffix_state = call(
        functools.partial(suffix_values_kernel, nz, local, group),
        "suffix_values",
        flat_state,
        (slot_branch, suffix_lengths, slot_values, probs, slot_lse, slot_inv),
        [SM, SM, VM, VM, VM, VM],
        vmem=8 << 20,
    )
    last = [received.pop(step) for step in groups[-1]]
    others = list(received.values())
    near = call(
        functools.partial(near_kernel, len(others), local, group, scale),
        "near",
        state,
        (joined, fresh, *suffix_state, own_out, own_lse, *others),
        [VM] * (6 + len(others)),
        moved=rows * head_dim * 20,
    )
    received = last
    pieces = call(
        functools.partial(final_kernel, len(received), local),
        "final",
        [jax.ShapeDtypeStruct((qrows, head_dim), BF16)] * nz,
        (*near, *received),
        [VM] * (2 + len(received)),
        moved=rows * head_dim * 20,
    )
    landed = [pieces[0]] + [
        shift(pieces[step], "branch", back(step, nz), nz) for step in range(nz - 1, 0, -1)
    ][::-1]
    out = call(
        functools.partial(unpack_kernel, nz, local, group),
        "unpack",
        jax.ShapeDtypeStruct((nb, nz, heads // nz, head_dim), BF16),
        landed[::-1],
        [VM] * nz,
        moved=queries.size * 4,
    )
    return out.reshape(nb, heads, head_dim)


def solution(mesh):
    lanes = P(("groups", "blk", "branch"), None, None)
    return jax.shard_map(
        functools.partial(per_device, mesh.shape["branch"], mesh.shape["blk"]),
        mesh=mesh,
        in_specs=(
            lanes,
            lanes,
            lanes,
            P(("groups", "blk"), "branch", None),
            P(("groups", "blk"), "branch", None),
            P(("groups", "blk"), None, "branch", None),
            P(("groups", "blk"), None, "branch", None),
            P("groups"),
            P("groups"),
        ),
        out_specs=lanes,
        check_vma=False,
    )
```

```python
import functools
import math

import jax
import jax.numpy as jnp
from jax import lax
from jax.experimental import pallas as pl
from jax.experimental.pallas import tpu as pltpu
from jax.sharding import PartitionSpec as P

NEG = -1e30
GAP = 1 << 36
CHUNK = 256
FOLD = 128
LOG2E = 1.4426950408889634
F32 = jnp.float32
BF16 = jnp.bfloat16
VM = pl.BlockSpec(memory_space=pltpu.VMEM)
SM = pl.BlockSpec(memory_space=pltpu.SMEM)
HBM = pl.BlockSpec(memory_space=pltpu.HBM)
NT = (((1,), (1,)), ((), ()))
NN = (((1,), (0,)), ((), ()))


def ceil_to(value, unit):
    return -(-value // unit) * unit


def partner(index, step, count):
    if count & (count - 1) == 0:
        return index ^ step
    return (index + step) % count


def back(step, count):
    return step if count & (count - 1) == 0 else (count - step) % count


def step_to(me, other, count):
    if count & (count - 1) == 0:
        return me ^ other
    return lax.rem(me - other + count, count)


def in_hbm(x):
    return pltpu.with_memory_space_constraint(x, pltpu.HBM)


def call(kernel, name, out_shape, inputs, in_specs, scratch=(), vmem=16 << 20, flops=0, moved=0, out_specs=None):
    many = isinstance(out_shape, (list, tuple))
    return pl.pallas_call(
        kernel,
        name=name,
        out_shape=out_shape,
        in_specs=in_specs,
        out_specs=out_specs if out_specs is not None else ([VM] * len(out_shape) if many else VM),
        scratch_shapes=list(scratch),
        compiler_params=pltpu.CompilerParams(vmem_limit_bytes=vmem),
        cost_estimate=pl.CostEstimate(flops=flops, bytes_accessed=moved, transcendentals=0),
    )(*inputs)


def pack_kernel(nz, local, group, pad, q_hbm, k_hbm, v_hbm, *refs):
    out_refs, (q_ref, k_ref, v_ref, sems) = refs[:nz], refs[nz:]
    copies = [
        pltpu.make_async_copy(src, dst, sems.at[i])
        for i, (src, dst) in enumerate(((q_hbm, q_ref), (k_hbm, k_ref), (v_hbm, v_ref)))
    ]
    for copy in copies:
        copy.start()
    for copy in copies:
        copy.wait()
    me = lax.axis_index("branch")
    nb = q_ref.shape[0]
    head_dim = q_ref.shape[-1]
    new_k = k_ref[...].astype(F32)
    new_v = v_ref[...].astype(F32)
    for step in range(nz):
        peer = partner(me, step, nz)
        q = q_ref[:, peer].astype(F32)
        parts = [
            q[:, kl * group : (kl + 1) * group].reshape(nb * group, head_dim) for kl in range(local)
        ]
        rows_k, rows_v = new_k[:, :local], new_v[:, :local]
        for z in range(1, nz):
            here = peer == z
            rows_k = jnp.where(here, new_k[:, z * local : (z + 1) * local], rows_k)
            rows_v = jnp.where(here, new_v[:, z * local : (z + 1) * local], rows_v)
        for rows in (rows_k, rows_v):
            for kl in range(local):
                parts += [rows[b, kl : kl + 1] for b in range(nb)]
        if pad:
            parts.append(jnp.zeros((pad, head_dim), F32))
        out_refs[step][...] = jnp.concatenate(parts, axis=0).astype(BF16)


def join_kernel(order, qrows, *refs):
    q_ref, tail_ref, all_ref = refs[-3:]
    for at, step in enumerate(order):
        q_ref[step] = refs[at][:qrows]
        tail_ref[step] = refs[at][qrows:]
        all_ref[step] = refs[at][...]


def gap_kernel(after, token):
    token[...] = jnp.zeros(token.shape, token.dtype)


def split_kernel(local, pk, pv, pko, pvo, token, wide):
    token[...] = jnp.zeros(token.shape, token.dtype)
    chunk = wide.shape[0]
    rows = chunk // local
    for src, dst in ((pk, pko), (pv, pvo)):
        for at in range(src.shape[0] // chunk):
            wide[...] = src[at * chunk : (at + 1) * chunk].astype(F32)
            for kl in range(local):
                head = wide[pl.ds(kl, rows, stride=local)] if local > 1 else wide[...]
                if dst is pvo:
                    dst[kl, :, at * rows : (at + 1) * rows] = head.T.astype(BF16)
                else:
                    dst[kl, at * rows : (at + 1) * rows] = head.astype(BF16)


def places(c, slots, nz, local, group, slot_ref, len_ref):
    first = lax.axis_index("blk") * slots
    branch = slot_ref[first + c]
    length = len_ref[branch]
    branch = branch - first
    nb = slots // nz
    step = step_to(lax.axis_index("branch"), branch // nb, nz)
    at = step * (nb * group) + lax.rem(branch, nb) * group
    return [pl.multiple_of(at + kl * (slots * group), 8) for kl in range(local)], length


def suffix_kernel(
    nz, local, group, scale, q_ref, slot_ref, len_ref, keys, values, out_ref, lse_ref, qwide, scores, probs
):
    slots, width, head_dim = keys.shape
    part = slots // nz * group
    for step in range(nz):
        for kl in range(local):
            at = kl * nz * part + step * part
            qwide[at : at + part] = q_ref[step, kl * part : (kl + 1) * part].astype(F32)
    heads = local * group
    column = lax.broadcasted_iota(jnp.int32, (heads, width), 1)
    row = lax.broadcasted_iota(jnp.int32, (heads, width), 0)
    own_head = lax.rem(column, local) == row // group
    for c in range(slots):
        at, length = places(c, slots, nz, local, group, slot_ref, len_ref)
        q = jnp.concatenate([qwide[pl.ds(a, group)] for a in at], axis=0).astype(BF16)
        s = lax.dot_general(q, keys[c], NT, preferred_element_type=F32)
        scores[c * heads : (c + 1) * heads] = jnp.where(
            own_head & (column < length * local), s, NEG
        )
    s = scores[...]
    top = jnp.max(s, axis=-1, keepdims=True)
    weights = jnp.exp2((s - top) * (scale * LOG2E))
    total = jnp.sum(weights, axis=-1, keepdims=True)
    probs[...] = weights.astype(BF16)
    lse = top * scale + jnp.log(total)
    inverse = 1.0 / total
    for c in range(slots):
        at, _ = places(c, slots, nz, local, group, slot_ref, len_ref)
        o = jnp.dot(probs[c * heads : (c + 1) * heads], values[c], preferred_element_type=F32)
        o = o * inverse[c * heads : (c + 1) * heads]
        for kl in range(local):
            lo, hi = kl * group, (kl + 1) * group
            out_ref[pl.ds(at[kl], group)] = o[lo:hi]
            lse_ref[pl.ds(at[kl], group)] = jnp.broadcast_to(
                lse[c * heads + lo : c * heads + hi], (group, head_dim)
            )


def encode(outs, lses):
    rows = jnp.concatenate(lses, axis=0)
    high = rows.astype(BF16).astype(F32)
    middle = (rows - high).astype(BF16).astype(F32)
    low = rows - high - middle
    used = 3 * rows.shape[0]
    pad = jnp.zeros((ceil_to(used, 16) - used, rows.shape[1]), F32)
    return jnp.concatenate([*outs, high, middle, low, pad], axis=0).astype(BF16)


def decode(payload, local):
    wide = payload.astype(F32)
    count = wide.shape[0] - ceil_to(3 * local, 16)
    size = count // local
    parts = []
    for kl in range(local):
        high, middle, low = (wide[count + i * local + kl :][:1] for i in range(3))
        parts.append((wide[kl * size : (kl + 1) * size], high + middle + low))
    return parts


def merge(parts):
    top = parts[0][1]
    for _, lse in parts[1:]:
        top = jnp.maximum(top, lse)
    weights = [jnp.exp2((lse - top) * LOG2E) for _, lse in parts]
    total = sum(weights[1:], weights[0])
    inverse = 1.0 / total
    out = parts[0][0] * (weights[0] * inverse)
    for (o, _), w in zip(parts[1:], weights[1:]):
        out = out + o * (w * inverse)
    return out, top + jnp.log(total)


def keys_as_rows(qs, k_ref, v_ref, scale):
    positions, width = k_ref.shape[1], qs[0].shape[0]
    chunk = math.gcd(positions, CHUNK)
    fold = math.gcd(chunk, FOLD)

    def folded(x, reduce):
        return reduce(x.reshape(chunk // fold, fold, width), axis=0)

    pieces = [slice(at, at + chunk) for at in range(0, positions, chunk)]
    scores, tops = [], []
    for kl, q in enumerate(qs):
        scores.append(
            [lax.dot_general(k_ref[kl, p], q, NT, preferred_element_type=F32) for p in pieces]
        )
        top = folded(scores[kl][0], jnp.max)
        for s in scores[kl][1:]:
            top = jnp.maximum(top, folded(s, jnp.max))
        tops.append(jnp.max(top, axis=0, keepdims=True))
    heads = []
    for kl in range(len(qs)):
        total, out = 0.0, 0.0
        for p, s in zip(pieces, scores[kl]):
            weights = jnp.exp2((s - tops[kl]) * (scale * LOG2E))
            total = total + folded(weights, jnp.sum)
            out = out + lax.dot_general(
                v_ref[kl, :, p], weights.astype(BF16), NN, preferred_element_type=F32
            )
        total = jnp.sum(total, axis=0, keepdims=True)
        heads.append((out * (1.0 / total), tops[kl] * scale + jnp.log(total)))
    return heads


def queries_as_rows(qs, k_ref, v_ref, scale):
    scores = [
        lax.dot_general(q, k_ref[kl], NT, preferred_element_type=F32) for kl, q in enumerate(qs)
    ]
    parts = []
    for s in scores:
        top = jnp.max(s, axis=1, keepdims=True)
        weights = jnp.exp2((s - top) * (scale * LOG2E))
        parts.append((top, jnp.sum(weights, axis=1, keepdims=True), weights.astype(BF16)))
    heads = []
    for kl, (top, total, weights) in enumerate(parts):
        out = lax.dot_general(weights, v_ref[kl], NT, preferred_element_type=F32) * (1.0 / total)
        lse = jnp.broadcast_to(top * scale + jnp.log(total), out.shape)
        heads.append((out.T, lse.T[:1]))
    return heads


def prefix_kernel(count, own, merged, local, part, scale, *refs):
    q_refs, (k_ref, v_ref), refs = refs[:count], refs[count : count + 2], refs[count + 2 :]
    others, outs = (refs[:count], refs[count:]) if merged else ((), refs)
    steps, part = q_refs[0].shape[0], part // local
    columns = steps * part
    qs = [
        jnp.concatenate(
            [ref[z, kl * part : (kl + 1) * part] for ref in q_refs for z in range(steps)], axis=0
        )
        for kl in range(local)
    ]
    heads = (keys_as_rows if count * columns > 128 else queries_as_rows)(qs, k_ref, v_ref, scale)
    for i in range(count):
        at = slice(i * columns, (i + 1) * columns)
        parts = [(o[:, at], lse[:, at]) for o, lse in heads]
        if merged:
            parts = [merge(pair) for pair in zip(parts, decode(others[i][...], local))]
        os, lses = zip(*parts)
        if own and i == count - 1:
            outs[i][...] = jnp.concatenate(os, axis=0)
            outs[i + 1][:local] = jnp.concatenate(lses, axis=0)
        else:
            outs[i][...] = encode(os, lses)


def near_kernel(count, local, group, scale, q_ref, fresh_ref, so_ref, sl_ref, po_ref, pl_ref, *refs):
    others, (out_ref, lse_ref) = refs[:count], refs[count:]
    nz, qrows = q_ref.shape[:2]
    part = qrows // local
    nb = part // group
    columns = nz * part
    head_dim = so_ref.shape[1]
    decoded = [decode(ref[...], local) for ref in others]
    for kl in range(local):
        scores, news = [], []
        for step in range(nz):
            q = q_ref[step, kl * part : (kl + 1) * part].astype(F32)
            tail = fresh_ref[step].astype(F32)
            k, v = (
                jnp.concatenate(
                    [
                        jnp.broadcast_to(tail[i : i + 1], (group, head_dim))
                        for i in range(at + kl * nb, at + (kl + 1) * nb)
                    ],
                    axis=0,
                )
                for at in (0, nb * local)
            )
            scores.append(jnp.sum(q * k, axis=1, keepdims=True) * scale)
            news.append(v)
        rows = slice(kl * columns, (kl + 1) * columns)
        out, lse = merge(
            [
                (jnp.concatenate(news, axis=0), jnp.concatenate(scores, axis=0)),
                (so_ref[rows], sl_ref[rows]),
            ]
        )
        at = slice(kl * head_dim, (kl + 1) * head_dim)
        parts = [(out.T, lse.T[:1]), (po_ref[at], pl_ref[kl : kl + 1])]
        out, lse = merge(parts + [d[kl] for d in decoded])
        out_ref[at] = out
        lse_ref[kl : kl + 1] = lse


def final_kernel(count, local, near_ref, lse_ref, *refs):
    others, outs = refs[:count], refs[count:]
    head_dim = near_ref.shape[0] // local
    part = outs[0].shape[0] // local
    decoded = [decode(ref[...], local) for ref in others]
    for kl in range(local):
        at = slice(kl * head_dim, (kl + 1) * head_dim)
        out, _ = merge([(near_ref[at], lse_ref[kl : kl + 1])] + [d[kl] for d in decoded])
        out = out.T
        for step, ref in enumerate(outs):
            ref[kl * part : (kl + 1) * part] = out[step * part : (step + 1) * part].astype(BF16)


def unpack_kernel(order, local, group, *refs):
    pieces, out_ref = refs[:-1], refs[-1]
    nz = len(order)
    me = lax.axis_index("branch")
    nb = out_ref.shape[0]
    for at, step in enumerate(order):
        peer = partner(me, step, nz)
        wide = pieces[at][...].astype(F32)
        for b in range(nb):
            rows = [wide[(kl * nb + b) * group : (kl * nb + b + 1) * group] for kl in range(local)]
            out_ref[b, peer] = jnp.concatenate(rows, axis=0).astype(BF16)


def per_device(
    nz, nblk, queries, new_keys, fresh_token_values, prefix_keys, prefix_values, suffix_keys,
    suffix_values, suffix_lengths, slot_branch
):
    nb, heads, head_dim = queries.shape
    positions, local = prefix_keys.shape[:2]
    group = heads // new_keys.shape[1]
    slots, suffix = suffix_keys.shape[:2]
    scale = 1.0 / math.sqrt(head_dim)
    qrows = local * nb * group
    used = qrows + 2 * nb * local
    padded = ceil_to(used, 16)
    rows = nz * qrows
    order_in = [*range(nz - 1, 0, -1), 0]
    order_out = order_in
    nc = 2 if nblk % 2 == 0 else 1
    nx = nblk // nc

    def shift(x, axis, step, count):
        return lax.ppermute(x, axis, [(i, partner(i, step, count)) for i in range(count)])

    def along_blk(x, step_x, step_c):
        return lax.ppermute(
            x,
            "blk",
            [
                (i, partner(i // nc, step_x, nx) * nc + partner(i % nc, step_c, nc))
                for i in range(nblk)
            ],
        )

    payloads = call(
        functools.partial(pack_kernel, nz, local, group, padded - used),
        "pack",
        [pltpu.VMEM((padded, head_dim), BF16)] * nz,
        (
            in_hbm(queries.reshape(nb, nz, heads // nz, head_dim)),
            in_hbm(new_keys), in_hbm(fresh_token_values),
        ),
        [HBM] * 3,
        scratch=[
            pltpu.VMEM((nb, nz, heads // nz, head_dim), BF16),
            pltpu.VMEM(new_keys.shape, BF16),
            pltpu.VMEM(new_keys.shape, BF16),
            pltpu.SemaphoreType.DMA((3,)),
        ],
        moved=queries.size * 4,
    )
    gap = call(
        gap_kernel, "gap", pltpu.VMEM((8, head_dim), F32), (payloads[0],), [VM], flops=GAP, moved=GAP,
    )
    payloads, gap = lax.optimization_barrier((payloads, gap))
    arrived = [payloads[0]] + [
        shift(payloads[step], "branch", step, nz) for step in range(nz - 1, 0, -1)
    ][::-1]
    chunk = math.gcd(positions * local, 1024)
    flat = (positions * local, head_dim)
    width = suffix * local
    slot_rows = (slots, width, head_dim)
    slot_keys, slot_values = suffix_keys.reshape(slot_rows), suffix_values.reshape(slot_rows)
    keys, values, token = call(
        functools.partial(split_kernel, local),
        "split",
        [
            pltpu.VMEM((local, positions, head_dim), BF16),
            pltpu.VMEM((local, head_dim, positions), BF16),
            pltpu.VMEM((8, head_dim), F32),
        ],
        (prefix_keys.reshape(flat), prefix_values.reshape(flat)),
        [VM] * 2,
        scratch=[pltpu.VMEM((chunk, head_dim), F32)],
        vmem=8 << 20,
        moved=prefix_keys.size * 8,
    )
    joined, fresh, wide = call(
        functools.partial(join_kernel, order_in, qrows),
        "join",
        [
            jax.ShapeDtypeStruct((nz, qrows, head_dim), BF16),
            jax.ShapeDtypeStruct((nz, padded - qrows, head_dim), BF16),
            jax.ShapeDtypeStruct((nz, padded, head_dim), BF16),
        ],
        (*[arrived[step] for step in order_in], gap, token),
        [VM] * (nz + 2),
        moved=nz * padded * head_dim * 4,
    )

    columns = rows // local
    state = [
        jax.ShapeDtypeStruct((local * head_dim, columns), F32),
        jax.ShapeDtypeStruct((ceil_to(local, 8), columns), F32),
    ]
    payload = jax.ShapeDtypeStruct((local * head_dim + ceil_to(3 * local, 16), columns), BF16)

    def prefix(name, arrays, own=False, others=()):
        count = len(arrays)
        return call(
            functools.partial(prefix_kernel, count, own, bool(others), local, qrows, scale),
            name,
            [payload] * (count - own) + (state if own else []),
            (*arrays, keys, values, *others),
            [VM] * (count + 2 + len(others)),
            vmem=16 << 20,
            flops=4 * count * rows * positions * head_dim if own else 0,
            moved=keys.size * 4 if own else 0,
        )

    far_steps = [(x, c) for x in range(1, nx) for c in range(nc)]
    near_steps = [(0, c) for c in range(1, nc)]
    arriving = {step: along_blk(joined if step[1] else wide, *step) for step in far_steps + near_steps}

    def give_back(x, step):
        return along_blk(x, back(step[0], nx), back(step[1], nc))

    rows_of = [arriving[step] for step in near_steps]
    *sent, own_out, own_lse = prefix("prefix_near", [*rows_of, joined], own=True)
    received = {step: give_back(x, step) for x, step in zip(sent, near_steps)}
    sibling = list(received.values())
    distant = []
    for far in range(1, nx):
        hopped = []
        for core in range(nc - 1, -1, -1):
            rows_of, own_lse = lax.optimization_barrier((arriving[far, core], own_lse))
            (sent,) = prefix("prefix_far", [rows_of], others=() if core else hopped)
            if core:
                hopped.append(give_back(sent, (0, core)))
            else:
                distant.append(give_back(sent, (far, 0)))
            sent, own_lse = lax.optimization_barrier((sent, own_lse))
    own_lse, slot_keys = lax.optimization_barrier((own_lse, slot_keys))
    suffix_state = call(
        functools.partial(suffix_kernel, nz, local, group, scale),
        "suffix",
        [jax.ShapeDtypeStruct((rows, head_dim), F32)] * 2,
        (joined, slot_branch, suffix_lengths, slot_keys, slot_values),
        [VM, SM, SM, VM, VM],
        scratch=[
            pltpu.VMEM((rows, head_dim), F32),
            pltpu.VMEM((slots * local * group, width), F32),
            pltpu.VMEM((slots * local * group, width), BF16),
        ],
        vmem=8 << 20,
    )
    near = call(
        functools.partial(near_kernel, len(sibling), local, group, scale),
        "near",
        state,
        (joined, fresh, *suffix_state, own_out, own_lse, *sibling),
        [VM] * (6 + len(sibling)),
        moved=rows * head_dim * 20,
    )
    pieces = call(
        functools.partial(final_kernel, len(distant), local),
        "final",
        [jax.ShapeDtypeStruct((qrows, head_dim), BF16)] * nz,
        (*near, *distant),
        [VM] * (2 + len(distant)),
        moved=rows * head_dim * 20,
    )
    landed = [pieces[0]] + [
        shift(pieces[step], "branch", back(step, nz), nz) for step in range(nz - 1, 0, -1)
    ][::-1]
    out = call(
        functools.partial(unpack_kernel, order_out, local, group),
        "unpack",
        jax.ShapeDtypeStruct((nb, nz, heads // nz, head_dim), BF16),
        [landed[step] for step in order_out],
        [VM] * nz,
        moved=queries.size * 4,
    )
    return out.reshape(nb, heads, head_dim)


def solution(mesh):
    lanes = P(("groups", "blk", "branch"), None, None)
    return jax.shard_map(
        functools.partial(per_device, mesh.shape["branch"], mesh.shape["blk"]),
        mesh=mesh,
        in_specs=(
            lanes,
            lanes,
            lanes,
            P(("groups", "blk"), "branch", None),
            P(("groups", "blk"), "branch", None),
            P(("groups", "blk"), None, "branch", None),
            P(("groups", "blk"), None, "branch", None),
            P("groups"),
            P("groups"),
        ),
        out_specs=lanes,
        check_vma=False,
    )
```

```python
import functools
import math

import jax
import jax.numpy as jnp
from jax import lax
from jax.experimental import pallas as pl
from jax.experimental.pallas import tpu as pltpu
from jax.sharding import PartitionSpec as P

NEG = -1e30
GAP = 1 << 36
LOG2E = 1.4426950408889634
F32 = jnp.float32
BF16 = jnp.bfloat16
VM = pl.BlockSpec(memory_space=pltpu.VMEM)
SM = pl.BlockSpec(memory_space=pltpu.SMEM)
HBM = pl.BlockSpec(memory_space=pltpu.HBM)
NT = (((1,), (1,)), ((), ()))


def ceil_to(value, unit):
    return -(-value // unit) * unit


def partner(index, step, count):
    if count & (count - 1) == 0:
        return index ^ step
    return (index + step) % count


def back(step, count):
    return step if count & (count - 1) == 0 else (count - step) % count


def step_to(me, other, count):
    if count & (count - 1) == 0:
        return me ^ other
    return lax.rem(me - other + count, count)


def in_hbm(x):
    return pltpu.with_memory_space_constraint(x, pltpu.HBM)


def call(kernel, name, out_shape, inputs, in_specs, scratch=(), vmem=16 << 20, flops=0, moved=0, out_specs=None):
    many = isinstance(out_shape, (list, tuple))
    return pl.pallas_call(
        kernel,
        name=name,
        out_shape=out_shape,
        in_specs=in_specs,
        out_specs=out_specs if out_specs is not None else ([VM] * len(out_shape) if many else VM),
        scratch_shapes=list(scratch),
        compiler_params=pltpu.CompilerParams(vmem_limit_bytes=vmem),
        cost_estimate=pl.CostEstimate(flops=flops, bytes_accessed=moved, transcendentals=0),
    )(*inputs)


def pack_kernel(nz, local, group, pad, q_hbm, k_hbm, v_hbm, *refs):
    out_refs, (q_ref, k_ref, v_ref, sems) = refs[:nz], refs[nz:]
    copies = [
        pltpu.make_async_copy(src, dst, sems.at[i])
        for i, (src, dst) in enumerate(((q_hbm, q_ref), (k_hbm, k_ref), (v_hbm, v_ref)))
    ]
    for copy in copies:
        copy.start()
    for copy in copies:
        copy.wait()
    me = lax.axis_index("branch")
    nb = q_ref.shape[0]
    head_dim = q_ref.shape[-1]
    new_k = k_ref[...].astype(F32)
    new_v = v_ref[...].astype(F32)
    for step in range(nz):
        peer = partner(me, step, nz)
        q = q_ref[:, peer].astype(F32)
        parts = [
            q[:, kl * group : (kl + 1) * group].reshape(nb * group, head_dim) for kl in range(local)
        ]
        rows_k, rows_v = new_k[:, :local], new_v[:, :local]
        for z in range(1, nz):
            here = peer == z
            rows_k = jnp.where(here, new_k[:, z * local : (z + 1) * local], rows_k)
            rows_v = jnp.where(here, new_v[:, z * local : (z + 1) * local], rows_v)
        for rows in (rows_k, rows_v):
            for kl in range(local):
                parts += [rows[b, kl : kl + 1] for b in range(nb)]
        if pad:
            parts.append(jnp.zeros((pad, head_dim), F32))
        out_refs[step][...] = jnp.concatenate(parts, axis=0).astype(BF16)


def join_kernel(order, qrows, *refs):
    q_ref, tail_ref, all_ref = refs[-3:]
    for at, step in enumerate(order):
        q_ref[step] = refs[at][:qrows]
        tail_ref[step] = refs[at][qrows:]
        all_ref[step] = refs[at][...]


def gap_kernel(after, token):
    token[...] = jnp.zeros(token.shape, token.dtype)


def split_kernel(local, pk, pv, pko, pvo, token, wide):
    token[...] = jnp.zeros(token.shape, token.dtype)
    chunk = wide.shape[0]
    rows = chunk // local
    for src, dst in ((pk, pko), (pv, pvo)):
        for at in range(src.shape[0] // chunk):
            wide[...] = src[at * chunk : (at + 1) * chunk].astype(F32)
            for kl in range(local):
                head = wide[pl.ds(kl, rows, stride=local)] if local > 1 else wide[...]
                dst[kl, at * rows : (at + 1) * rows] = head.astype(BF16)


def places(c, slots, nz, local, group, slot_ref, len_ref):
    first = lax.axis_index("blk") * slots
    branch = slot_ref[first + c]
    length = len_ref[branch]
    branch = branch - first
    nb = slots // nz
    step = step_to(lax.axis_index("branch"), branch // nb, nz)
    at = step * (nb * group) + lax.rem(branch, nb) * group
    return [pl.multiple_of(at + kl * (slots * group), 8) for kl in range(local)], length


def suffix_kernel(
    nz, local, group, scale, q_ref, slot_ref, len_ref, keys, values, out_ref, lse_ref, qwide, scores, probs
):
    slots, width, head_dim = keys.shape
    part = slots // nz * group
    for step in range(nz):
        for kl in range(local):
            at = kl * nz * part + step * part
            qwide[at : at + part] = q_ref[step, kl * part : (kl + 1) * part].astype(F32)
    heads = local * group
    column = lax.broadcasted_iota(jnp.int32, (heads, width), 1)
    row = lax.broadcasted_iota(jnp.int32, (heads, width), 0)
    own_head = lax.rem(column, local) == row // group
    for c in range(slots):
        at, length = places(c, slots, nz, local, group, slot_ref, len_ref)
        q = jnp.concatenate([qwide[pl.ds(a, group)] for a in at], axis=0).astype(BF16)
        s = lax.dot_general(q, keys[c], NT, preferred_element_type=F32)
        scores[c * heads : (c + 1) * heads] = jnp.where(
            own_head & (column < length * local), s, NEG
        )
    s = scores[...]
    top = jnp.max(s, axis=-1, keepdims=True)
    weights = jnp.exp2((s - top) * (scale * LOG2E))
    total = jnp.sum(weights, axis=-1, keepdims=True)
    probs[...] = weights.astype(BF16)
    lse = top * scale + jnp.log(total)
    inverse = 1.0 / total
    for c in range(slots):
        at, _ = places(c, slots, nz, local, group, slot_ref, len_ref)
        o = jnp.dot(probs[c * heads : (c + 1) * heads], values[c], preferred_element_type=F32)
        o = o * inverse[c * heads : (c + 1) * heads]
        for kl in range(local):
            lo, hi = kl * group, (kl + 1) * group
            out_ref[pl.ds(at[kl], group)] = o[lo:hi]
            lse_ref[pl.ds(at[kl], group)] = jnp.broadcast_to(
                lse[c * heads + lo : c * heads + hi], (group, head_dim)
            )


def encode(outs, lses):
    rows = jnp.concatenate(lses, axis=0)
    high = rows.astype(BF16).astype(F32)
    middle = (rows - high).astype(BF16).astype(F32)
    low = rows - high - middle
    used = 3 * rows.shape[0]
    pad = jnp.zeros((ceil_to(used, 16) - used, rows.shape[1]), F32)
    return jnp.concatenate([*outs, high, middle, low, pad], axis=0).astype(BF16)


def decode(payload, local):
    wide = payload.astype(F32)
    count = wide.shape[0] - ceil_to(3 * local, 16)
    size = count // local
    parts = []
    for kl in range(local):
        high, middle, low = (wide[count + i * local + kl :][:1] for i in range(3))
        parts.append((wide[kl * size : (kl + 1) * size], high + middle + low))
    return parts


def merge(parts):
    top = parts[0][1]
    for _, lse in parts[1:]:
        top = jnp.maximum(top, lse)
    weights = [jnp.exp2((lse - top) * LOG2E) for _, lse in parts]
    total = sum(weights[1:], weights[0])
    inverse = 1.0 / total
    out = parts[0][0] * (weights[0] * inverse)
    for (o, _), w in zip(parts[1:], weights[1:]):
        out = out + o * (w * inverse)
    return out, top + jnp.log(total)


def attend(qs, k_ref, v_ref, scale):
    scores = [
        lax.dot_general(q, k_ref[kl], NT, preferred_element_type=F32) for kl, q in enumerate(qs)
    ]
    parts = []
    for s in scores:
        top = jnp.max(s, axis=1, keepdims=True)
        weights = jnp.exp2((s - top) * (scale * LOG2E))
        parts.append((top, jnp.sum(weights, axis=1, keepdims=True), weights.astype(BF16)))
    heads = []
    for kl, (top, total, weights) in enumerate(parts):
        out = jnp.dot(weights, v_ref[kl], preferred_element_type=F32) * (1.0 / total)
        lse = jnp.broadcast_to(top * scale + jnp.log(total), out.shape)
        heads.append((out.T, lse.T))
    return heads


def prefix_kernel(count, own, merged, local, part, scale, *refs):
    q_refs, (k_ref, v_ref), refs = refs[:count], refs[count : count + 2], refs[count + 2 :]
    others, outs = (refs[:count], refs[count:]) if merged else ((), refs)
    steps, part = q_refs[0].shape[0], part // local
    columns = steps * part
    qs = [
        jnp.concatenate(
            [ref[z, kl * part : (kl + 1) * part] for ref in q_refs for z in range(steps)], axis=0
        )
        for kl in range(local)
    ]
    heads = attend(qs, k_ref, v_ref, scale)
    for i in range(count):
        at = slice(i * columns, (i + 1) * columns)
        parts = [(o[:, at], lse[:1, at]) for o, lse in heads]
        if merged:
            parts = [merge(pair) for pair in zip(parts, decode(others[i][...], local))]
        os, lses = zip(*parts)
        if own and i == count - 1:
            outs[i][...] = jnp.concatenate(os, axis=0)
            outs[i + 1][:local] = jnp.concatenate(lses, axis=0)
        else:
            outs[i][...] = encode(os, lses)


def near_kernel(count, local, group, scale, q_ref, fresh_ref, so_ref, sl_ref, po_ref, pl_ref, *refs):
    others, (out_ref, lse_ref) = refs[:count], refs[count:]
    nz, qrows = q_ref.shape[:2]
    part = qrows // local
    nb = part // group
    columns = nz * part
    head_dim = so_ref.shape[1]
    decoded = [decode(ref[...], local) for ref in others]
    for kl in range(local):
        scores, news = [], []
        for step in range(nz):
            q = q_ref[step, kl * part : (kl + 1) * part].astype(F32)
            tail = fresh_ref[step].astype(F32)
            k, v = (
                jnp.concatenate(
                    [
                        jnp.broadcast_to(tail[i : i + 1], (group, head_dim))
                        for i in range(at + kl * nb, at + (kl + 1) * nb)
                    ],
                    axis=0,
                )
                for at in (0, nb * local)
            )
            scores.append(jnp.sum(q * k, axis=1, keepdims=True) * scale)
            news.append(v)
        rows = slice(kl * columns, (kl + 1) * columns)
        out, lse = merge(
            [
                (jnp.concatenate(news, axis=0), jnp.concatenate(scores, axis=0)),
                (so_ref[rows], sl_ref[rows]),
            ]
        )
        at = slice(kl * head_dim, (kl + 1) * head_dim)
        parts = [(out.T, lse.T[:1]), (po_ref[at], pl_ref[kl : kl + 1])]
        out, lse = merge(parts + [d[kl] for d in decoded])
        out_ref[at] = out
        lse_ref[kl : kl + 1] = lse


def final_kernel(count, local, near_ref, lse_ref, *refs):
    others, outs = refs[:count], refs[count:]
    head_dim = near_ref.shape[0] // local
    part = outs[0].shape[0] // local
    decoded = [decode(ref[...], local) for ref in others]
    for kl in range(local):
        at = slice(kl * head_dim, (kl + 1) * head_dim)
        out, _ = merge([(near_ref[at], lse_ref[kl : kl + 1])] + [d[kl] for d in decoded])
        out = out.T
        for step, ref in enumerate(outs):
            ref[kl * part : (kl + 1) * part] = out[step * part : (step + 1) * part].astype(BF16)


def unpack_kernel(order, local, group, *refs):
    pieces, out_ref = refs[:-1], refs[-1]
    nz = len(order)
    me = lax.axis_index("branch")
    nb = out_ref.shape[0]
    for at, step in enumerate(order):
        peer = partner(me, step, nz)
        wide = pieces[at][...].astype(F32)
        for b in range(nb):
            rows = [wide[(kl * nb + b) * group : (kl * nb + b + 1) * group] for kl in range(local)]
            out_ref[b, peer] = jnp.concatenate(rows, axis=0).astype(BF16)


def per_device(
    nz, nblk, queries, new_keys, fresh_token_values, prefix_keys, prefix_values, suffix_keys,
    suffix_values, suffix_lengths, slot_branch
):
    nb, heads, head_dim = queries.shape
    positions, local = prefix_keys.shape[:2]
    group = heads // new_keys.shape[1]
    slots, suffix = suffix_keys.shape[:2]
    scale = 1.0 / math.sqrt(head_dim)
    qrows = local * nb * group
    used = qrows + 2 * nb * local
    padded = ceil_to(used, 16)
    rows = nz * qrows
    order = [*range(nz - 1, 0, -1), 0]
    nc = 2 if nblk % 2 == 0 else 1
    nx = nblk // nc

    def shift(x, axis, step, count):
        return lax.ppermute(x, axis, [(i, partner(i, step, count)) for i in range(count)])

    def along_blk(x, step_x, step_c):
        return lax.ppermute(
            x,
            "blk",
            [
                (i, partner(i // nc, step_x, nx) * nc + partner(i % nc, step_c, nc))
                for i in range(nblk)
            ],
        )

    payloads = call(
        functools.partial(pack_kernel, nz, local, group, padded - used),
        "pack",
        [pltpu.VMEM((padded, head_dim), BF16)] * nz,
        (
            in_hbm(queries.reshape(nb, nz, heads // nz, head_dim)),
            in_hbm(new_keys), in_hbm(fresh_token_values),
        ),
        [HBM] * 3,
        scratch=[
            pltpu.VMEM((nb, nz, heads // nz, head_dim), BF16),
            pltpu.VMEM(new_keys.shape, BF16),
            pltpu.VMEM(new_keys.shape, BF16),
            pltpu.SemaphoreType.DMA((3,)),
        ],
        moved=queries.size * 4,
    )
    gap = call(
        gap_kernel, "gap", pltpu.VMEM((8, head_dim), F32), (payloads[0],), [VM], flops=GAP, moved=GAP,
    )
    payloads, gap = lax.optimization_barrier((payloads, gap))
    arrived = [payloads[0]] + [
        shift(payloads[step], "branch", step, nz) for step in range(nz - 1, 0, -1)
    ][::-1]
    chunk = math.gcd(positions * local, 1024)
    flat = (positions * local, head_dim)
    width = suffix * local
    slot_rows = (slots, width, head_dim)
    slot_keys, slot_values = suffix_keys.reshape(slot_rows), suffix_values.reshape(slot_rows)
    keys, values, token = call(
        functools.partial(split_kernel, local),
        "split",
        [pltpu.VMEM((local, positions, head_dim), BF16)] * 2 + [pltpu.VMEM((8, head_dim), F32)],
        (prefix_keys.reshape(flat), prefix_values.reshape(flat)),
        [VM] * 2,
        scratch=[pltpu.VMEM((chunk, head_dim), F32)],
        vmem=8 << 20,
        moved=prefix_keys.size * 8,
    )
    joined, fresh, wide = call(
        functools.partial(join_kernel, order, qrows),
        "join",
        [
            jax.ShapeDtypeStruct((nz, qrows, head_dim), BF16),
            jax.ShapeDtypeStruct((nz, padded - qrows, head_dim), BF16),
            jax.ShapeDtypeStruct((nz, padded, head_dim), BF16),
        ],
        (*[arrived[step] for step in order], gap, token),
        [VM] * (nz + 2),
        moved=nz * padded * head_dim * 4,
    )

    columns = rows // local
    state = [
        jax.ShapeDtypeStruct((local * head_dim, columns), F32),
        jax.ShapeDtypeStruct((ceil_to(local, 8), columns), F32),
    ]
    payload = jax.ShapeDtypeStruct((local * head_dim + ceil_to(3 * local, 16), columns), BF16)

    def prefix(name, arrays, own=False, others=()):
        count = len(arrays)
        return call(
            functools.partial(prefix_kernel, count, own, bool(others), local, qrows, scale),
            name,
            [payload] * (count - own) + (state if own else []),
            (*arrays, keys, values, *others),
            [VM] * (count + 2 + len(others)),
            vmem=16 << 20,
            flops=4 * count * rows * positions * head_dim if own else 0,
            moved=keys.size * 4 if own else 0,
        )

    far_steps = [(x, c) for x in range(1, nx) for c in range(nc)]
    near_steps = [(0, c) for c in range(1, nc)]
    arriving = {step: along_blk(joined if step[1] else wide, *step) for step in far_steps + near_steps}

    def give_back(x, step):
        return along_blk(x, back(step[0], nx), back(step[1], nc))

    rows_of = [arriving[step] for step in near_steps]
    *sent, own_out, own_lse = prefix("prefix_near", [*rows_of, joined], own=True)
    received = {step: give_back(x, step) for x, step in zip(sent, near_steps)}
    sibling = list(received.values())
    distant = []
    for far in range(1, nx):
        hopped = []
        for core in range(nc - 1, -1, -1):
            rows_of, own_lse = lax.optimization_barrier((arriving[far, core], own_lse))
            (sent,) = prefix("prefix_far", [rows_of], others=() if core else hopped)
            if core:
                hopped.append(give_back(sent, (0, core)))
            else:
                distant.append(give_back(sent, (far, 0)))
            sent, own_lse = lax.optimization_barrier((sent, own_lse))
    own_lse, slot_keys = lax.optimization_barrier((own_lse, slot_keys))
    suffix_state = call(
        functools.partial(suffix_kernel, nz, local, group, scale),
        "suffix",
        [jax.ShapeDtypeStruct((rows, head_dim), F32)] * 2,
        (joined, slot_branch, suffix_lengths, slot_keys, slot_values),
        [VM, SM, SM, VM, VM],
        scratch=[
            pltpu.VMEM((rows, head_dim), F32),
            pltpu.VMEM((slots * local * group, width), F32),
            pltpu.VMEM((slots * local * group, width), BF16),
        ],
        vmem=8 << 20,
    )
    near = call(
        functools.partial(near_kernel, len(sibling), local, group, scale),
        "near",
        state,
        (joined, fresh, *suffix_state, own_out, own_lse, *sibling),
        [VM] * (6 + len(sibling)),
        moved=rows * head_dim * 20,
    )
    pieces = call(
        functools.partial(final_kernel, len(distant), local),
        "final",
        [jax.ShapeDtypeStruct((qrows, head_dim), BF16)] * nz,
        (*near, *distant),
        [VM] * (2 + len(distant)),
        moved=rows * head_dim * 20,
    )
    landed = [pieces[0]] + [
        shift(pieces[step], "branch", back(step, nz), nz) for step in range(nz - 1, 0, -1)
    ][::-1]
    out = call(
        functools.partial(unpack_kernel, order, local, group),
        "unpack",
        jax.ShapeDtypeStruct((nb, nz, heads // nz, head_dim), BF16),
        [landed[step] for step in order],
        [VM] * nz,
        moved=queries.size * 4,
    )
    return out.reshape(nb, heads, head_dim)


def solution(mesh):
    lanes = P(("groups", "blk", "branch"), None, None)
    return jax.shard_map(
        functools.partial(per_device, mesh.shape["branch"], mesh.shape["blk"]),
        mesh=mesh,
        in_specs=(
            lanes,
            lanes,
            lanes,
            P(("groups", "blk"), "branch", None),
            P(("groups", "blk"), "branch", None),
            P(("groups", "blk"), None, "branch", None),
            P(("groups", "blk"), None, "branch", None),
            P("groups"),
            P("groups"),
        ),
        out_specs=lanes,
        check_vma=False,
    )
```

```python
import functools
import math

import jax
import jax.numpy as jnp
from jax import lax
from jax.experimental import pallas as pl
from jax.experimental.pallas import tpu as pltpu
from jax.sharding import PartitionSpec as P

NEG = -1e30
GAP = 1 << 36
LOG2E = 1.4426950408889634
F32 = jnp.float32
BF16 = jnp.bfloat16
VM = pl.BlockSpec(memory_space=pltpu.VMEM)
SM = pl.BlockSpec(memory_space=pltpu.SMEM)
HBM = pl.BlockSpec(memory_space=pltpu.HBM)
NT = (((1,), (1,)), ((), ()))


def ceil_to(value, unit):
    return -(-value // unit) * unit


def partner(index, step, count):
    if count & (count - 1) == 0:
        return index ^ step
    return (index + step) % count


def back(step, count):
    return step if count & (count - 1) == 0 else (count - step) % count


def step_to(me, other, count):
    if count & (count - 1) == 0:
        return me ^ other
    return lax.rem(me - other + count, count)


def in_hbm(x):
    return pltpu.with_memory_space_constraint(x, pltpu.HBM)


def call(kernel, name, out_shape, inputs, in_specs, scratch=(), vmem=16 << 20, flops=0, moved=0, out_specs=None):
    many = isinstance(out_shape, (list, tuple))
    return pl.pallas_call(
        kernel,
        name=name,
        out_shape=out_shape,
        in_specs=in_specs,
        out_specs=out_specs if out_specs is not None else ([VM] * len(out_shape) if many else VM),
        scratch_shapes=list(scratch),
        compiler_params=pltpu.CompilerParams(vmem_limit_bytes=vmem),
        cost_estimate=pl.CostEstimate(flops=flops, bytes_accessed=moved, transcendentals=0),
    )(*inputs)


def pack_kernel(nz, local, group, pad, q_hbm, k_hbm, v_hbm, *refs):
    out_refs, (q_ref, k_ref, v_ref, sems) = refs[:nz], refs[nz:]
    copies = [
        pltpu.make_async_copy(src, dst, sems.at[i])
        for i, (src, dst) in enumerate(((q_hbm, q_ref), (k_hbm, k_ref), (v_hbm, v_ref)))
    ]
    for copy in copies:
        copy.start()
    for copy in copies:
        copy.wait()
    me = lax.axis_index("branch")
    nb = q_ref.shape[0]
    head_dim = q_ref.shape[-1]
    new_k = k_ref[...].astype(F32)
    new_v = v_ref[...].astype(F32)
    for step in range(nz):
        peer = partner(me, step, nz)
        q = q_ref[:, peer].astype(F32)
        parts = [
            q[:, kl * group : (kl + 1) * group].reshape(nb * group, head_dim) for kl in range(local)
        ]
        rows_k, rows_v = new_k[:, :local], new_v[:, :local]
        for z in range(1, nz):
            here = peer == z
            rows_k = jnp.where(here, new_k[:, z * local : (z + 1) * local], rows_k)
            rows_v = jnp.where(here, new_v[:, z * local : (z + 1) * local], rows_v)
        for rows in (rows_k, rows_v):
            for kl in range(local):
                parts += [rows[b, kl : kl + 1] for b in range(nb)]
        if pad:
            parts.append(jnp.zeros((pad, head_dim), F32))
        out_refs[step][...] = jnp.concatenate(parts, axis=0).astype(BF16)


def join_kernel(order, qrows, *refs):
    q_ref, tail_ref = refs[-2:]
    for at, step in enumerate(order):
        q_ref[step] = refs[at][:qrows]
        tail_ref[step] = refs[at][qrows:]


def gap_kernel(after, token):
    token[...] = jnp.zeros(token.shape, token.dtype)


def split_kernel(local, pk, pv, pko, pvo, token, wide):
    token[...] = jnp.zeros(token.shape, token.dtype)
    chunk = wide.shape[0]
    rows = chunk // local
    for src, dst in ((pk, pko), (pv, pvo)):
        for at in range(src.shape[0] // chunk):
            wide[...] = src[at * chunk : (at + 1) * chunk].astype(F32)
            for kl in range(local):
                head = wide[pl.ds(kl, rows, stride=local)] if local > 1 else wide[...]
                dst[kl, at * rows : (at + 1) * rows] = head.astype(BF16)


def places(c, slots, nz, local, group, slot_ref, len_ref):
    first = lax.axis_index("blk") * slots
    branch = slot_ref[first + c]
    length = len_ref[branch]
    branch = branch - first
    nb = slots // nz
    step = step_to(lax.axis_index("branch"), branch // nb, nz)
    at = step * (nb * group) + lax.rem(branch, nb) * group
    return [pl.multiple_of(at + kl * (slots * group), 8) for kl in range(local)], length


def suffix_kernel(
    nz, local, group, scale, q_ref, slot_ref, len_ref, keys, values, out_ref, lse_ref, qwide, scores, probs
):
    slots, width, head_dim = keys.shape
    part = slots // nz * group
    for step in range(nz):
        for kl in range(local):
            at = kl * nz * part + step * part
            qwide[at : at + part] = q_ref[step, kl * part : (kl + 1) * part].astype(F32)
    heads = local * group
    column = lax.broadcasted_iota(jnp.int32, (heads, width), 1)
    row = lax.broadcasted_iota(jnp.int32, (heads, width), 0)
    own_head = lax.rem(column, local) == row // group
    for c in range(slots):
        at, length = places(c, slots, nz, local, group, slot_ref, len_ref)
        q = jnp.concatenate([qwide[pl.ds(a, group)] for a in at], axis=0).astype(BF16)
        s = lax.dot_general(q, keys[c], NT, preferred_element_type=F32)
        scores[c * heads : (c + 1) * heads] = jnp.where(
            own_head & (column < length * local), s, NEG
        )
    s = scores[...]
    top = jnp.max(s, axis=-1, keepdims=True)
    weights = jnp.exp2((s - top) * (scale * LOG2E))
    total = jnp.sum(weights, axis=-1, keepdims=True)
    probs[...] = weights.astype(BF16)
    lse = top * scale + jnp.log(total)
    inverse = 1.0 / total
    for c in range(slots):
        at, _ = places(c, slots, nz, local, group, slot_ref, len_ref)
        o = jnp.dot(probs[c * heads : (c + 1) * heads], values[c], preferred_element_type=F32)
        o = o * inverse[c * heads : (c + 1) * heads]
        for kl in range(local):
            lo, hi = kl * group, (kl + 1) * group
            out_ref[pl.ds(at[kl], group)] = o[lo:hi]
            lse_ref[pl.ds(at[kl], group)] = jnp.broadcast_to(
                lse[c * heads + lo : c * heads + hi], (group, head_dim)
            )


def encode(outs, lses):
    rows = jnp.concatenate(lses, axis=0)
    high = rows.astype(BF16).astype(F32)
    middle = (rows - high).astype(BF16).astype(F32)
    low = rows - high - middle
    used = 3 * rows.shape[0]
    pad = jnp.zeros((ceil_to(used, 16) - used, rows.shape[1]), F32)
    return jnp.concatenate([*outs, high, middle, low, pad], axis=0).astype(BF16)


def decode(payload, local):
    wide = payload.astype(F32)
    count = wide.shape[0] - ceil_to(3 * local, 16)
    size = count // local
    parts = []
    for kl in range(local):
        high, middle, low = (wide[count + i * local + kl :][:1] for i in range(3))
        parts.append((wide[kl * size : (kl + 1) * size], high + middle + low))
    return parts


def merge(parts):
    top = parts[0][1]
    for _, lse in parts[1:]:
        top = jnp.maximum(top, lse)
    weights = [jnp.exp2((lse - top) * LOG2E) for _, lse in parts]
    total = sum(weights[1:], weights[0])
    inverse = 1.0 / total
    out = parts[0][0] * (weights[0] * inverse)
    for (o, _), w in zip(parts[1:], weights[1:]):
        out = out + o * (w * inverse)
    return out, top + jnp.log(total)


def attend(qs, k_ref, v_ref, scale):
    scores = [
        lax.dot_general(q, k_ref[kl], NT, preferred_element_type=F32) for kl, q in enumerate(qs)
    ]
    parts = []
    for s in scores:
        top = jnp.max(s, axis=1, keepdims=True)
        weights = jnp.exp2((s - top) * (scale * LOG2E))
        parts.append((top, jnp.sum(weights, axis=1, keepdims=True), weights.astype(BF16)))
    heads = []
    for kl, (top, total, weights) in enumerate(parts):
        out = jnp.dot(weights, v_ref[kl], preferred_element_type=F32) * (1.0 / total)
        lse = jnp.broadcast_to(top * scale + jnp.log(total), out.shape)
        heads.append((out.T, lse.T))
    return heads


def prefix_kernel(count, own, local, part, scale, *refs):
    q_refs, (k_ref, v_ref), outs = refs[:count], refs[count : count + 2], refs[count + 2 :]
    steps, part = q_refs[0].shape[0], part // local
    columns = steps * part
    qs = [
        jnp.concatenate(
            [ref[z, kl * part : (kl + 1) * part] for ref in q_refs for z in range(steps)], axis=0
        )
        for kl in range(local)
    ]
    heads = attend(qs, k_ref, v_ref, scale)
    for i in range(count):
        at = slice(i * columns, (i + 1) * columns)
        os, lses = zip(*((o[:, at], lse[:1, at]) for o, lse in heads))
        if own and i == count - 1:
            outs[i][...] = jnp.concatenate(os, axis=0)
            outs[i + 1][:local] = jnp.concatenate(lses, axis=0)
        else:
            outs[i][...] = encode(os, lses)


def join_partials_kernel(local, o_ref, lse_ref, other_ref, out_ref):
    size = o_ref.shape[0] // local
    parts = [
        merge([(o_ref[kl * size : (kl + 1) * size], lse_ref[kl : kl + 1]), other])
        for kl, other in enumerate(decode(other_ref[...], local))
    ]
    out_ref[...] = encode(*zip(*parts))


def near_kernel(count, local, group, scale, q_ref, fresh_ref, so_ref, sl_ref, po_ref, pl_ref, *refs):
    others, (out_ref, lse_ref) = refs[:count], refs[count:]
    nz, qrows = q_ref.shape[:2]
    part = qrows // local
    nb = part // group
    columns = nz * part
    head_dim = so_ref.shape[1]
    decoded = [decode(ref[...], local) for ref in others]
    for kl in range(local):
        scores, news = [], []
        for step in range(nz):
            q = q_ref[step, kl * part : (kl + 1) * part].astype(F32)
            tail = fresh_ref[step].astype(F32)
            k, v = (
                jnp.concatenate(
                    [
                        jnp.broadcast_to(tail[i : i + 1], (group, head_dim))
                        for i in range(at + kl * nb, at + (kl + 1) * nb)
                    ],
                    axis=0,
                )
                for at in (0, nb * local)
            )
            scores.append(jnp.sum(q * k, axis=1, keepdims=True) * scale)
            news.append(v)
        rows = slice(kl * columns, (kl + 1) * columns)
        out, lse = merge(
            [
                (jnp.concatenate(news, axis=0), jnp.concatenate(scores, axis=0)),
                (so_ref[rows], sl_ref[rows]),
            ]
        )
        at = slice(kl * head_dim, (kl + 1) * head_dim)
        parts = [(out.T, lse.T[:1]), (po_ref[at], pl_ref[kl : kl + 1])]
        out, lse = merge(parts + [d[kl] for d in decoded])
        out_ref[at] = out
        lse_ref[kl : kl + 1] = lse


def final_kernel(count, local, near_ref, lse_ref, *refs):
    others, outs = refs[:count], refs[count:]
    head_dim = near_ref.shape[0] // local
    part = outs[0].shape[0] // local
    decoded = [decode(ref[...], local) for ref in others]
    for kl in range(local):
        at = slice(kl * head_dim, (kl + 1) * head_dim)
        out, _ = merge([(near_ref[at], lse_ref[kl : kl + 1])] + [d[kl] for d in decoded])
        out = out.T
        for step, ref in enumerate(outs):
            ref[kl * part : (kl + 1) * part] = out[step * part : (step + 1) * part].astype(BF16)


def unpack_kernel(order, local, group, *refs):
    pieces, out_ref = refs[:-1], refs[-1]
    nz = len(order)
    me = lax.axis_index("branch")
    nb = out_ref.shape[0]
    for at, step in enumerate(order):
        peer = partner(me, step, nz)
        wide = pieces[at][...].astype(F32)
        for b in range(nb):
            rows = [wide[(kl * nb + b) * group : (kl * nb + b + 1) * group] for kl in range(local)]
            out_ref[b, peer] = jnp.concatenate(rows, axis=0).astype(BF16)


def per_device(
    nz, nblk, queries, new_keys, fresh_token_values, prefix_keys, prefix_values, suffix_keys,
    suffix_values, suffix_lengths, slot_branch
):
    nb, heads, head_dim = queries.shape
    positions, local = prefix_keys.shape[:2]
    group = heads // new_keys.shape[1]
    slots, suffix = suffix_keys.shape[:2]
    scale = 1.0 / math.sqrt(head_dim)
    qrows = local * nb * group
    used = qrows + 2 * nb * local
    padded = ceil_to(used, 16)
    rows = nz * qrows
    order = [*range(nz - 1, 0, -1), 0]
    nc = 2 if nblk % 2 == 0 else 1
    nx = nblk // nc

    def shift(x, axis, step, count):
        return lax.ppermute(x, axis, [(i, partner(i, step, count)) for i in range(count)])

    def along_blk(x, step_x, step_c):
        return lax.ppermute(
            x,
            "blk",
            [
                (i, partner(i // nc, step_x, nx) * nc + partner(i % nc, step_c, nc))
                for i in range(nblk)
            ],
        )

    payloads = call(
        functools.partial(pack_kernel, nz, local, group, padded - used),
        "pack",
        [pltpu.VMEM((padded, head_dim), BF16)] * nz,
        (
            in_hbm(queries.reshape(nb, nz, heads // nz, head_dim)),
            in_hbm(new_keys), in_hbm(fresh_token_values),
        ),
        [HBM] * 3,
        scratch=[
            pltpu.VMEM((nb, nz, heads // nz, head_dim), BF16),
            pltpu.VMEM(new_keys.shape, BF16),
            pltpu.VMEM(new_keys.shape, BF16),
            pltpu.SemaphoreType.DMA((3,)),
        ],
        moved=queries.size * 4,
    )
    gap = call(
        gap_kernel, "gap", pltpu.VMEM((8, head_dim), F32), (payloads[0],), [VM], flops=GAP, moved=GAP,
    )
    payloads, gap = lax.optimization_barrier((payloads, gap))
    arrived = [payloads[0]] + [
        shift(payloads[step], "branch", step, nz) for step in range(nz - 1, 0, -1)
    ][::-1]
    chunk = math.gcd(positions * local, 1024)
    flat = (positions * local, head_dim)
    width = suffix * local
    slot_rows = (slots, width, head_dim)
    slot_keys, slot_values = suffix_keys.reshape(slot_rows), suffix_values.reshape(slot_rows)
    keys, values, token = call(
        functools.partial(split_kernel, local),
        "split",
        [pltpu.VMEM((local, positions, head_dim), BF16)] * 2 + [pltpu.VMEM((8, head_dim), F32)],
        (prefix_keys.reshape(flat), prefix_values.reshape(flat)),
        [VM] * 2,
        scratch=[pltpu.VMEM((chunk, head_dim), F32)],
        vmem=8 << 20,
        moved=prefix_keys.size * 8,
    )
    joined, fresh = call(
        functools.partial(join_kernel, order, qrows),
        "join",
        [
            jax.ShapeDtypeStruct((nz, qrows, head_dim), BF16),
            jax.ShapeDtypeStruct((nz, padded - qrows, head_dim), BF16),
        ],
        (*[arrived[step] for step in order], gap, token),
        [VM] * (nz + 2),
        moved=nz * padded * head_dim * 4,
    )

    columns = rows // local
    state = [
        jax.ShapeDtypeStruct((local * head_dim, columns), F32),
        jax.ShapeDtypeStruct((ceil_to(local, 8), columns), F32),
    ]
    payload = jax.ShapeDtypeStruct((local * head_dim + ceil_to(3 * local, 16), columns), BF16)

    def prefix(name, arrays, own=False):
        count = len(arrays)
        return call(
            functools.partial(prefix_kernel, count, own, local, qrows, scale),
            name,
            [payload] * (count - own) + (state if own else []),
            (*arrays, keys, values),
            [VM] * (count + 2),
            vmem=16 << 20,
            flops=4 * count * rows * positions * head_dim,
            moved=keys.size * 4,
        )

    near_steps = [(0, c) for c in range(1, nc)]
    arriving = {
        step: along_blk(joined, *step) for step in [(x, nc - 1) for x in range(1, nx)] + near_steps
    }

    def give_back(x, step):
        return along_blk(x, back(step[0], nx), back(step[1], nc))

    rows_of = [arriving[step] for step in near_steps]
    *sent, own_out, own_lse = prefix("prefix_near", [*rows_of, joined], own=True)
    received = {step: give_back(x, step) for x, step in zip(sent, near_steps)}
    sibling = list(received.values())
    distant = []
    for far in range(1, nx):
        rows_of, own_lse = lax.optimization_barrier((arriving[far, nc - 1], own_lse))
        (sent,) = prefix("prefix_far", [rows_of])
        if nc > 1:
            hopped = give_back(sent, (0, 1))
            rows_of, own_lse = lax.optimization_barrier(
                (along_blk(arriving[far, nc - 1], 0, 1), own_lse)
            )
            rows_of, sent = lax.optimization_barrier((rows_of, sent))
            partial = prefix("prefix_x", [rows_of], own=True)
            sent = call(
                functools.partial(join_partials_kernel, local),
                "join_partials",
                payload,
                (*partial, hopped),
                [VM] * 3,
            )
        distant.append(give_back(sent, (far, 0)))
        sent, own_lse = lax.optimization_barrier((sent, own_lse))
    own_lse, slot_keys = lax.optimization_barrier((own_lse, slot_keys))
    suffix_state = call(
        functools.partial(suffix_kernel, nz, local, group, scale),
        "suffix",
        [jax.ShapeDtypeStruct((rows, head_dim), F32)] * 2,
        (joined, slot_branch, suffix_lengths, slot_keys, slot_values),
        [VM, SM, SM, VM, VM],
        scratch=[
            pltpu.VMEM((rows, head_dim), F32),
            pltpu.VMEM((slots * local * group, width), F32),
            pltpu.VMEM((slots * local * group, width), BF16),
        ],
        vmem=8 << 20,
    )
    near = call(
        functools.partial(near_kernel, len(sibling), local, group, scale),
        "near",
        state,
        (joined, fresh, *suffix_state, own_out, own_lse, *sibling),
        [VM] * (6 + len(sibling)),
        moved=rows * head_dim * 20,
    )
    pieces = call(
        functools.partial(final_kernel, len(distant), local),
        "final",
        [jax.ShapeDtypeStruct((qrows, head_dim), BF16)] * nz,
        (*near, *distant),
        [VM] * (2 + len(distant)),
        moved=rows * head_dim * 20,
    )
    landed = [pieces[0]] + [
        shift(pieces[step], "branch", back(step, nz), nz) for step in range(nz - 1, 0, -1)
    ][::-1]
    out = call(
        functools.partial(unpack_kernel, order, local, group),
        "unpack",
        jax.ShapeDtypeStruct((nb, nz, heads // nz, head_dim), BF16),
        [landed[step] for step in order],
        [VM] * nz,
        moved=queries.size * 4,
    )
    return out.reshape(nb, heads, head_dim)


def solution(mesh):
    lanes = P(("groups", "blk", "branch"), None, None)
    return jax.shard_map(
        functools.partial(per_device, mesh.shape["branch"], mesh.shape["blk"]),
        mesh=mesh,
        in_specs=(
            lanes,
            lanes,
            lanes,
            P(("groups", "blk"), "branch", None),
            P(("groups", "blk"), "branch", None),
            P(("groups", "blk"), None, "branch", None),
            P(("groups", "blk"), None, "branch", None),
            P("groups"),
            P("groups"),
        ),
        out_specs=lanes,
        check_vma=False,
    )
```

```python
import functools
import math

import jax
import jax.numpy as jnp
from jax import lax
from jax.experimental import pallas as pl
from jax.experimental.pallas import tpu as pltpu
from jax.sharding import PartitionSpec as P

NEG = -1e30
GAP = 1 << 36
LOG2E = 1.4426950408889634
F32 = jnp.float32
BF16 = jnp.bfloat16
VM = pl.BlockSpec(memory_space=pltpu.VMEM)
SM = pl.BlockSpec(memory_space=pltpu.SMEM)
HBM = pl.BlockSpec(memory_space=pltpu.HBM)
NT = (((1,), (1,)), ((), ()))


def ceil_to(value, unit):
    return -(-value // unit) * unit


def partner(index, step, count):
    if count & (count - 1) == 0:
        return index ^ step
    return (index + step) % count


def back(step, count):
    return step if count & (count - 1) == 0 else (count - step) % count


def step_to(me, other, count):
    if count & (count - 1) == 0:
        return me ^ other
    return lax.rem(me - other + count, count)


def in_hbm(x):
    return pltpu.with_memory_space_constraint(x, pltpu.HBM)


def call(kernel, name, out_shape, inputs, in_specs, scratch=(), vmem=16 << 20, flops=0, moved=0, out_specs=None):
    many = isinstance(out_shape, (list, tuple))
    return pl.pallas_call(
        kernel,
        name=name,
        out_shape=out_shape,
        in_specs=in_specs,
        out_specs=out_specs if out_specs is not None else ([VM] * len(out_shape) if many else VM),
        scratch_shapes=list(scratch),
        compiler_params=pltpu.CompilerParams(vmem_limit_bytes=vmem),
        cost_estimate=pl.CostEstimate(flops=flops, bytes_accessed=moved, transcendentals=0),
    )(*inputs)


def pack_kernel(nz, local, group, pad, q_hbm, k_hbm, v_hbm, *refs):
    out_refs, (q_ref, k_ref, v_ref, sems) = refs[:nz], refs[nz:]
    copies = [
        pltpu.make_async_copy(src, dst, sems.at[i])
        for i, (src, dst) in enumerate(((q_hbm, q_ref), (k_hbm, k_ref), (v_hbm, v_ref)))
    ]
    for copy in copies:
        copy.start()
    for copy in copies:
        copy.wait()
    me = lax.axis_index("branch")
    nb = q_ref.shape[0]
    head_dim = q_ref.shape[-1]
    new_k = k_ref[...].astype(F32)
    new_v = v_ref[...].astype(F32)
    for step in range(nz):
        peer = partner(me, step, nz)
        q = q_ref[:, peer].astype(F32)
        parts = [
            q[:, kl * group : (kl + 1) * group].reshape(nb * group, head_dim) for kl in range(local)
        ]
        rows_k, rows_v = new_k[:, :local], new_v[:, :local]
        for z in range(1, nz):
            here = peer == z
            rows_k = jnp.where(here, new_k[:, z * local : (z + 1) * local], rows_k)
            rows_v = jnp.where(here, new_v[:, z * local : (z + 1) * local], rows_v)
        for rows in (rows_k, rows_v):
            for kl in range(local):
                parts += [rows[b, kl : kl + 1] for b in range(nb)]
        if pad:
            parts.append(jnp.zeros((pad, head_dim), F32))
        out_refs[step][...] = jnp.concatenate(parts, axis=0).astype(BF16)


def join_kernel(order, qrows, *refs):
    q_ref, tail_ref = refs[-2:]
    for at, step in enumerate(order):
        q_ref[step] = refs[at][:qrows]
        tail_ref[step] = refs[at][qrows:]


def gap_kernel(after, token):
    token[...] = jnp.zeros(token.shape, token.dtype)


def split_kernel(local, pk, pv, pko, pvo, token, wide):
    token[...] = jnp.zeros(token.shape, token.dtype)
    chunk = wide.shape[0]
    rows = chunk // local
    for src, dst in ((pk, pko), (pv, pvo)):
        for at in range(src.shape[0] // chunk):
            wide[...] = src[at * chunk : (at + 1) * chunk].astype(F32)
            for kl in range(local):
                head = wide[pl.ds(kl, rows, stride=local)] if local > 1 else wide[...]
                dst[kl, at * rows : (at + 1) * rows] = head.astype(BF16)


def places(c, slots, nz, local, group, slot_ref, len_ref):
    first = lax.axis_index("blk") * slots
    branch = slot_ref[first + c]
    length = len_ref[branch]
    branch = branch - first
    nb = slots // nz
    step = step_to(lax.axis_index("branch"), branch // nb, nz)
    at = step * (nb * group) + lax.rem(branch, nb) * group
    return [pl.multiple_of(at + kl * (slots * group), 8) for kl in range(local)], length


def suffix_kernel(
    nz, local, group, scale, q_ref, slot_ref, len_ref, keys, values, out_ref, lse_ref, qwide, scores, probs
):
    slots, width, head_dim = keys.shape
    part = slots // nz * group
    for step in range(nz):
        for kl in range(local):
            at = kl * nz * part + step * part
            qwide[at : at + part] = q_ref[step, kl * part : (kl + 1) * part].astype(F32)
    heads = local * group
    column = lax.broadcasted_iota(jnp.int32, (heads, width), 1)
    row = lax.broadcasted_iota(jnp.int32, (heads, width), 0)
    own_head = lax.rem(column, local) == row // group
    for c in range(slots):
        at, length = places(c, slots, nz, local, group, slot_ref, len_ref)
        q = jnp.concatenate([qwide[pl.ds(a, group)] for a in at], axis=0).astype(BF16)
        s = lax.dot_general(q, keys[c], NT, preferred_element_type=F32)
        scores[c * heads : (c + 1) * heads] = jnp.where(
            own_head & (column < length * local), s, NEG
        )
    s = scores[...]
    top = jnp.max(s, axis=-1, keepdims=True)
    weights = jnp.exp2((s - top) * (scale * LOG2E))
    total = jnp.sum(weights, axis=-1, keepdims=True)
    probs[...] = weights.astype(BF16)
    lse = top * scale + jnp.log(total)
    inverse = 1.0 / total
    for c in range(slots):
        at, _ = places(c, slots, nz, local, group, slot_ref, len_ref)
        o = jnp.dot(probs[c * heads : (c + 1) * heads], values[c], preferred_element_type=F32)
        o = o * inverse[c * heads : (c + 1) * heads]
        for kl in range(local):
            lo, hi = kl * group, (kl + 1) * group
            out_ref[pl.ds(at[kl], group)] = o[lo:hi]
            lse_ref[pl.ds(at[kl], group)] = jnp.broadcast_to(
                lse[c * heads + lo : c * heads + hi], (group, head_dim)
            )


def encode(outs, lses):
    rows = jnp.concatenate(lses, axis=0)
    high = rows.astype(BF16).astype(F32)
    middle = (rows - high).astype(BF16).astype(F32)
    low = rows - high - middle
    used = 3 * rows.shape[0]
    pad = jnp.zeros((ceil_to(used, 16) - used, rows.shape[1]), F32)
    return jnp.concatenate([*outs, high, middle, low, pad], axis=0).astype(BF16)


def decode(payload, local):
    wide = payload.astype(F32)
    count = wide.shape[0] - ceil_to(3 * local, 16)
    size = count // local
    parts = []
    for kl in range(local):
        high, middle, low = (wide[count + i * local + kl :][:1] for i in range(3))
        parts.append((wide[kl * size : (kl + 1) * size], high + middle + low))
    return parts


def merge(parts):
    top = parts[0][1]
    for _, lse in parts[1:]:
        top = jnp.maximum(top, lse)
    weights = [jnp.exp2((lse - top) * LOG2E) for _, lse in parts]
    total = sum(weights[1:], weights[0])
    inverse = 1.0 / total
    out = parts[0][0] * (weights[0] * inverse)
    for (o, _), w in zip(parts[1:], weights[1:]):
        out = out + o * (w * inverse)
    return out, top + jnp.log(total)


def attend(qs, k_ref, v_ref, scale):
    scores = [
        lax.dot_general(q, k_ref[kl], NT, preferred_element_type=F32) for kl, q in enumerate(qs)
    ]
    parts = []
    for s in scores:
        top = jnp.max(s, axis=1, keepdims=True)
        weights = jnp.exp2((s - top) * (scale * LOG2E))
        parts.append((top, jnp.sum(weights, axis=1, keepdims=True), weights.astype(BF16)))
    heads = []
    for kl, (top, total, weights) in enumerate(parts):
        out = jnp.dot(weights, v_ref[kl], preferred_element_type=F32) * (1.0 / total)
        lse = jnp.broadcast_to(top * scale + jnp.log(total), out.shape)
        heads.append((out.T, lse.T))
    return heads


def prefix_kernel(count, own, extra, local, part, scale, *refs):
    q_refs, (k_ref, v_ref), refs = refs[:count], refs[count : count + 2], refs[count + 2 :]
    extras, outs = refs[:extra], refs[extra:]
    steps, part = q_refs[0].shape[0], part // local
    columns = steps * part
    qs = [
        jnp.concatenate(
            [ref[z, kl * part : (kl + 1) * part] for ref in q_refs for z in range(steps)], axis=0
        )
        for kl in range(local)
    ]
    heads = attend(qs, k_ref, v_ref, scale)
    for i in range(count):
        at = slice(i * columns, (i + 1) * columns)
        os, lses = zip(*((o[:, at], lse[:1, at]) for o, lse in heads))
        if own and i == count - 1:
            outs[i][...] = jnp.concatenate(os, axis=0)
            outs[i + 1][:local] = jnp.concatenate(lses, axis=0)
        elif extra:
            size = extras[0].shape[0]
            outs[i][:size] = encode(os, lses)
            outs[i][size:] = extras[0][...]
        else:
            outs[i][...] = encode(os, lses)


def join_partials_kernel(local, o_ref, lse_ref, other_ref, out_ref):
    size = o_ref.shape[0] // local
    parts = [
        merge([(o_ref[kl * size : (kl + 1) * size], lse_ref[kl : kl + 1]), other])
        for kl, other in enumerate(decode(other_ref[: out_ref.shape[0]], local))
    ]
    out_ref[...] = encode(*zip(*parts))


def near_kernel(count, size, local, group, scale, q_ref, fresh_ref, so_ref, sl_ref, po_ref, pl_ref, *refs):
    others, (out_ref, lse_ref) = refs[:count], refs[count:]
    nz, qrows = q_ref.shape[:2]
    part = qrows // local
    nb = part // group
    columns = nz * part
    head_dim = so_ref.shape[1]
    decoded = [decode(ref[ref.shape[0] - size :], local) for ref in others]
    for kl in range(local):
        scores, news = [], []
        for step in range(nz):
            q = q_ref[step, kl * part : (kl + 1) * part].astype(F32)
            tail = fresh_ref[step].astype(F32)
            k, v = (
                jnp.concatenate(
                    [
                        jnp.broadcast_to(tail[i : i + 1], (group, head_dim))
                        for i in range(at + kl * nb, at + (kl + 1) * nb)
                    ],
                    axis=0,
                )
                for at in (0, nb * local)
            )
            scores.append(jnp.sum(q * k, axis=1, keepdims=True) * scale)
            news.append(v)
        rows = slice(kl * columns, (kl + 1) * columns)
        out, lse = merge(
            [
                (jnp.concatenate(news, axis=0), jnp.concatenate(scores, axis=0)),
                (so_ref[rows], sl_ref[rows]),
            ]
        )
        at = slice(kl * head_dim, (kl + 1) * head_dim)
        parts = [(out.T, lse.T[:1]), (po_ref[at], pl_ref[kl : kl + 1])]
        out, lse = merge(parts + [d[kl] for d in decoded])
        out_ref[at] = out
        lse_ref[kl : kl + 1] = lse


def final_kernel(count, local, near_ref, lse_ref, *refs):
    others, outs = refs[:count], refs[count:]
    head_dim = near_ref.shape[0] // local
    part = outs[0].shape[0] // local
    decoded = [decode(ref[...], local) for ref in others]
    for kl in range(local):
        at = slice(kl * head_dim, (kl + 1) * head_dim)
        out, _ = merge([(near_ref[at], lse_ref[kl : kl + 1])] + [d[kl] for d in decoded])
        out = out.T
        for step, ref in enumerate(outs):
            ref[kl * part : (kl + 1) * part] = out[step * part : (step + 1) * part].astype(BF16)


def unpack_kernel(order, local, group, *refs):
    pieces, out_ref = refs[:-1], refs[-1]
    nz = len(order)
    me = lax.axis_index("branch")
    nb = out_ref.shape[0]
    for at, step in enumerate(order):
        peer = partner(me, step, nz)
        wide = pieces[at][...].astype(F32)
        for b in range(nb):
            rows = [wide[(kl * nb + b) * group : (kl * nb + b + 1) * group] for kl in range(local)]
            out_ref[b, peer] = jnp.concatenate(rows, axis=0).astype(BF16)


def per_device(
    nz, nblk, queries, new_keys, fresh_token_values, prefix_keys, prefix_values, suffix_keys,
    suffix_values, suffix_lengths, slot_branch
):
    nb, heads, head_dim = queries.shape
    positions, local = prefix_keys.shape[:2]
    group = heads // new_keys.shape[1]
    slots, suffix = suffix_keys.shape[:2]
    scale = 1.0 / math.sqrt(head_dim)
    qrows = local * nb * group
    used = qrows + 2 * nb * local
    padded = ceil_to(used, 16)
    rows = nz * qrows
    order = [*range(nz - 1, 0, -1), 0]
    nc = 2 if nblk % 2 == 0 else 1
    nx = nblk // nc

    def shift(x, axis, step, count):
        return lax.ppermute(x, axis, [(i, partner(i, step, count)) for i in range(count)])

    def along_blk(x, step_x, step_c):
        return lax.ppermute(
            x,
            "blk",
            [
                (i, partner(i // nc, step_x, nx) * nc + partner(i % nc, step_c, nc))
                for i in range(nblk)
            ],
        )

    payloads = call(
        functools.partial(pack_kernel, nz, local, group, padded - used),
        "pack",
        [pltpu.VMEM((padded, head_dim), BF16)] * nz,
        (
            in_hbm(queries.reshape(nb, nz, heads // nz, head_dim)),
            in_hbm(new_keys), in_hbm(fresh_token_values),
        ),
        [HBM] * 3,
        scratch=[
            pltpu.VMEM((nb, nz, heads // nz, head_dim), BF16),
            pltpu.VMEM(new_keys.shape, BF16),
            pltpu.VMEM(new_keys.shape, BF16),
            pltpu.SemaphoreType.DMA((3,)),
        ],
        moved=queries.size * 4,
    )
    gap = call(
        gap_kernel, "gap", pltpu.VMEM((8, head_dim), F32), (payloads[0],), [VM], flops=GAP, moved=GAP,
    )
    payloads, gap = lax.optimization_barrier((payloads, gap))
    arrived = [payloads[0]] + [
        shift(payloads[step], "branch", step, nz) for step in range(nz - 1, 0, -1)
    ][::-1]
    chunk = math.gcd(positions * local, 1024)
    flat = (positions * local, head_dim)
    width = suffix * local
    slot_rows = (slots, width, head_dim)
    slot_keys, slot_values = suffix_keys.reshape(slot_rows), suffix_values.reshape(slot_rows)
    keys, values, token = call(
        functools.partial(split_kernel, local),
        "split",
        [pltpu.VMEM((local, positions, head_dim), BF16)] * 2 + [pltpu.VMEM((8, head_dim), F32)],
        (prefix_keys.reshape(flat), prefix_values.reshape(flat)),
        [VM] * 2,
        scratch=[pltpu.VMEM((chunk, head_dim), F32)],
        vmem=8 << 20,
        moved=prefix_keys.size * 8,
    )
    joined, fresh = call(
        functools.partial(join_kernel, order, qrows),
        "join",
        [
            jax.ShapeDtypeStruct((nz, qrows, head_dim), BF16),
            jax.ShapeDtypeStruct((nz, padded - qrows, head_dim), BF16),
        ],
        (*[arrived[step] for step in order], gap, token),
        [VM] * (nz + 2),
        moved=nz * padded * head_dim * 4,
    )

    columns = rows // local
    state = [
        jax.ShapeDtypeStruct((local * head_dim, columns), F32),
        jax.ShapeDtypeStruct((ceil_to(local, 8), columns), F32),
    ]
    payload = jax.ShapeDtypeStruct((local * head_dim + ceil_to(3 * local, 16), columns), BF16)

    pair = jax.ShapeDtypeStruct((2 * payload.shape[0], columns), BF16)

    def prefix(name, arrays, own=False, extra=(), weight=1):
        count = len(arrays)
        sent = pair if extra else payload
        return call(
            functools.partial(prefix_kernel, count, own, len(extra), local, qrows, scale),
            name,
            [sent] * (count - own) + (state if own else []),
            (*arrays, keys, values, *extra),
            [VM] * (count + 2 + len(extra)),
            vmem=16 << 20,
            flops=4 * weight * count * rows * positions * head_dim,
            moved=4 * weight * keys.size,
        )

    near_steps = [(0, c) for c in range(1, nc)]
    arriving = {
        step: along_blk(joined, *step) for step in [(x, nc - 1) for x in range(1, nx)] + near_steps
    }

    def give_back(x, step):
        return along_blk(x, back(step[0], nx), back(step[1], nc))

    rows_of = [arriving[step] for step in near_steps]
    *sibling, own_out, own_lse = prefix("prefix_near", [*rows_of, joined], own=True)
    distant = []
    for far in range(1, nx):
        rows_of, own_lse = lax.optimization_barrier((arriving[far, nc - 1], own_lse))
        first = nc > 1 and far == 1
        (sent,) = prefix("prefix_far", [rows_of], extra=sibling if first else ())
        if nc > 1:
            hopped = give_back(sent, (0, 1))
            if first:
                sibling = [hopped]
            rows_of, own_lse = lax.optimization_barrier(
                (along_blk(arriving[far, nc - 1], 0, 1), own_lse)
            )
            rows_of, sent = lax.optimization_barrier((rows_of, sent))
            partial = prefix("prefix_x", [rows_of], own=True, weight=3)
            sent = call(
                functools.partial(join_partials_kernel, local),
                "join_partials",
                payload,
                (*partial, hopped),
                [VM] * 3,
            )
        distant.append(give_back(sent, (far, 0)))
        sent, own_lse = lax.optimization_barrier((sent, own_lse))
    if nx == 1:
        sibling = [give_back(x, step) for x, step in zip(sibling, near_steps)]
    own_lse, slot_keys = lax.optimization_barrier((own_lse, slot_keys))
    suffix_state = call(
        functools.partial(suffix_kernel, nz, local, group, scale),
        "suffix",
        [jax.ShapeDtypeStruct((rows, head_dim), F32)] * 2,
        (joined, slot_branch, suffix_lengths, slot_keys, slot_values),
        [VM, SM, SM, VM, VM],
        scratch=[
            pltpu.VMEM((rows, head_dim), F32),
            pltpu.VMEM((slots * local * group, width), F32),
            pltpu.VMEM((slots * local * group, width), BF16),
        ],
        vmem=8 << 20,
    )
    near = call(
        functools.partial(near_kernel, len(sibling), payload.shape[0], local, group, scale),
        "near",
        state,
        (joined, fresh, *suffix_state, own_out, own_lse, *sibling),
        [VM] * (6 + len(sibling)),
        moved=rows * head_dim * 20,
    )
    pieces = call(
        functools.partial(final_kernel, len(distant), local),
        "final",
        [jax.ShapeDtypeStruct((qrows, head_dim), BF16)] * nz,
        (*near, *distant),
        [VM] * (2 + len(distant)),
        moved=rows * head_dim * 20,
    )
    landed = [pieces[0]] + [
        shift(pieces[step], "branch", back(step, nz), nz) for step in range(nz - 1, 0, -1)
    ][::-1]
    out = call(
        functools.partial(unpack_kernel, order, local, group),
        "unpack",
        jax.ShapeDtypeStruct((nb, nz, heads // nz, head_dim), BF16),
        [landed[step] for step in order],
        [VM] * nz,
        moved=queries.size * 4,
    )
    return out.reshape(nb, heads, head_dim)


def solution(mesh):
    lanes = P(("groups", "blk", "branch"), None, None)
    return jax.shard_map(
        functools.partial(per_device, mesh.shape["branch"], mesh.shape["blk"]),
        mesh=mesh,
        in_specs=(
            lanes,
            lanes,
            lanes,
            P(("groups", "blk"), "branch", None),
            P(("groups", "blk"), "branch", None),
            P(("groups", "blk"), None, "branch", None),
            P(("groups", "blk"), None, "branch", None),
            P("groups"),
            P("groups"),
        ),
        out_specs=lanes,
        check_vma=False,
    )
```

```python
import functools
import math

import jax
import jax.numpy as jnp
from jax import lax
from jax.experimental import pallas as pl
from jax.experimental.pallas import tpu as pltpu
from jax.sharding import PartitionSpec as P

NEG = -1e30
GAP = 1 << 36
LOG2E = 1.4426950408889634
F32 = jnp.float32
BF16 = jnp.bfloat16
VM = pl.BlockSpec(memory_space=pltpu.VMEM)
SM = pl.BlockSpec(memory_space=pltpu.SMEM)
HBM = pl.BlockSpec(memory_space=pltpu.HBM)
NT = (((1,), (1,)), ((), ()))


def ceil_to(value, unit):
    return -(-value // unit) * unit


def partner(index, step, count):
    if count & (count - 1) == 0:
        return index ^ step
    return (index + step) % count


def back(step, count):
    return step if count & (count - 1) == 0 else (count - step) % count


def step_to(me, other, count):
    if count & (count - 1) == 0:
        return me ^ other
    return lax.rem(me - other + count, count)


def in_hbm(x):
    return pltpu.with_memory_space_constraint(x, pltpu.HBM)


def call(kernel, name, out_shape, inputs, in_specs, scratch=(), vmem=16 << 20, flops=0, moved=0, out_specs=None):
    many = isinstance(out_shape, (list, tuple))
    return pl.pallas_call(
        kernel,
        name=name,
        out_shape=out_shape,
        in_specs=in_specs,
        out_specs=out_specs if out_specs is not None else ([VM] * len(out_shape) if many else VM),
        scratch_shapes=list(scratch),
        compiler_params=pltpu.CompilerParams(vmem_limit_bytes=vmem),
        cost_estimate=pl.CostEstimate(flops=flops, bytes_accessed=moved, transcendentals=0),
    )(*inputs)


def pack_kernel(nz, local, group, pad, q_hbm, k_hbm, v_hbm, *refs):
    out_refs, (q_ref, k_ref, v_ref, sems) = refs[:nz], refs[nz:]
    pairs = [(q_hbm.at[b], q_ref.at[b]) for b in range(q_hbm.shape[0])]
    pairs += [(k_hbm, k_ref), (v_hbm, v_ref)]
    copies = [pltpu.make_async_copy(src, dst, sems.at[i]) for i, (src, dst) in enumerate(pairs)]
    for copy in copies:
        copy.start()
    for copy in copies:
        copy.wait()
    me = lax.axis_index("branch")
    nb = q_ref.shape[0]
    head_dim = q_ref.shape[-1]
    new_k = k_ref[...].astype(F32)
    new_v = v_ref[...].astype(F32)
    for step in range(nz):
        peer = partner(me, step, nz)
        q = q_ref[:, peer].astype(F32)
        parts = [
            q[:, kl * group : (kl + 1) * group].reshape(nb * group, head_dim) for kl in range(local)
        ]
        rows_k, rows_v = new_k[:, :local], new_v[:, :local]
        for z in range(1, nz):
            here = peer == z
            rows_k = jnp.where(here, new_k[:, z * local : (z + 1) * local], rows_k)
            rows_v = jnp.where(here, new_v[:, z * local : (z + 1) * local], rows_v)
        for rows in (rows_k, rows_v):
            for kl in range(local):
                parts += [rows[b, kl : kl + 1] for b in range(nb)]
        if pad:
            parts.append(jnp.zeros((pad, head_dim), F32))
        out_refs[step][...] = jnp.concatenate(parts, axis=0).astype(BF16)


def join_kernel(order, qrows, *refs):
    q_ref, tail_ref = refs[-2:]
    for at, step in enumerate(order):
        q_ref[step] = refs[at][:qrows]
        tail_ref[step] = refs[at][qrows:]


def gap_kernel(after, token):
    token[...] = jnp.zeros(token.shape, token.dtype)


def split_kernel(local, pk, pv, pko, pvo, token, wide):
    token[...] = jnp.zeros(token.shape, token.dtype)
    chunk = wide.shape[0]
    rows = chunk // local
    for src, dst in ((pk, pko), (pv, pvo)):
        for at in range(src.shape[0] // chunk):
            wide[...] = src[at * chunk : (at + 1) * chunk].astype(F32)
            for kl in range(local):
                head = wide[pl.ds(kl, rows, stride=local)] if local > 1 else wide[...]
                dst[kl, at * rows : (at + 1) * rows] = head.astype(BF16)


def places(c, slots, nz, local, group, slot_ref, len_ref):
    first = lax.axis_index("blk") * slots
    branch = slot_ref[first + c]
    length = len_ref[branch]
    branch = branch - first
    nb = slots // nz
    step = step_to(lax.axis_index("branch"), branch // nb, nz)
    at = step * (nb * group) + lax.rem(branch, nb) * group
    return [pl.multiple_of(at + kl * (slots * group), 8) for kl in range(local)], length


def suffix_kernel(
    nz, local, group, scale, q_ref, slot_ref, len_ref, keys, values, out_ref, lse_ref, qwide, scores, probs
):
    slots, width, head_dim = keys.shape
    part = slots // nz * group
    for step in range(nz):
        for kl in range(local):
            at = kl * nz * part + step * part
            qwide[at : at + part] = q_ref[step, kl * part : (kl + 1) * part].astype(F32)
    heads = local * group
    column = lax.broadcasted_iota(jnp.int32, (heads, width), 1)
    row = lax.broadcasted_iota(jnp.int32, (heads, width), 0)
    own_head = lax.rem(column, local) == row // group
    for c in range(slots):
        at, length = places(c, slots, nz, local, group, slot_ref, len_ref)
        q = jnp.concatenate([qwide[pl.ds(a, group)] for a in at], axis=0).astype(BF16)
        s = lax.dot_general(q, keys[c], NT, preferred_element_type=F32)
        scores[c * heads : (c + 1) * heads] = jnp.where(
            own_head & (column < length * local), s, NEG
        )
    s = scores[...]
    top = jnp.max(s, axis=-1, keepdims=True)
    weights = jnp.exp2((s - top) * (scale * LOG2E))
    total = jnp.sum(weights, axis=-1, keepdims=True)
    probs[...] = weights.astype(BF16)
    lse = top * scale + jnp.log(total)
    inverse = 1.0 / total
    for c in range(slots):
        at, _ = places(c, slots, nz, local, group, slot_ref, len_ref)
        o = jnp.dot(probs[c * heads : (c + 1) * heads], values[c], preferred_element_type=F32)
        o = o * inverse[c * heads : (c + 1) * heads]
        for kl in range(local):
            lo, hi = kl * group, (kl + 1) * group
            out_ref[pl.ds(at[kl], group)] = o[lo:hi]
            lse_ref[pl.ds(at[kl], group)] = jnp.broadcast_to(
                lse[c * heads + lo : c * heads + hi], (group, head_dim)
            )


def encode(outs, lses):
    rows = jnp.concatenate(lses, axis=0)
    high = rows.astype(BF16).astype(F32)
    middle = (rows - high).astype(BF16).astype(F32)
    low = rows - high - middle
    used = 3 * rows.shape[0]
    pad = jnp.zeros((ceil_to(used, 16) - used, rows.shape[1]), F32)
    return jnp.concatenate([*outs, high, middle, low, pad], axis=0).astype(BF16)


def decode(payload, local):
    wide = payload.astype(F32)
    count = wide.shape[0] - ceil_to(3 * local, 16)
    size = count // local
    parts = []
    for kl in range(local):
        high, middle, low = (wide[count + i * local + kl :][:1] for i in range(3))
        parts.append((wide[kl * size : (kl + 1) * size], high + middle + low))
    return parts


def merge(parts):
    top = parts[0][1]
    for _, lse in parts[1:]:
        top = jnp.maximum(top, lse)
    weights = [jnp.exp2((lse - top) * LOG2E) for _, lse in parts]
    total = sum(weights[1:], weights[0])
    inverse = 1.0 / total
    out = parts[0][0] * (weights[0] * inverse)
    for (o, _), w in zip(parts[1:], weights[1:]):
        out = out + o * (w * inverse)
    return out, top + jnp.log(total)


def attend(qs, k_ref, v_ref, scale):
    scores = [
        lax.dot_general(q, k_ref[kl], NT, preferred_element_type=F32) for kl, q in enumerate(qs)
    ]
    parts = []
    for s in scores:
        top = jnp.max(s, axis=1, keepdims=True)
        weights = jnp.exp2((s - top) * (scale * LOG2E))
        parts.append((top, jnp.sum(weights, axis=1, keepdims=True), weights.astype(BF16)))
    heads = []
    for kl, (top, total, weights) in enumerate(parts):
        out = jnp.dot(weights, v_ref[kl], preferred_element_type=F32) * (1.0 / total)
        lse = jnp.broadcast_to(top * scale + jnp.log(total), out.shape)
        heads.append((out.T, lse.T))
    return heads


def bundle_kernel(q_ref, payload_ref, out_ref):
    steps, qrows = q_ref.shape[:2]
    for z in range(steps):
        out_ref[z * qrows : (z + 1) * qrows] = q_ref[z]
    out_ref[steps * qrows :] = payload_ref[...]


def prefix_kernel(count, own, steps, local, part, scale, *refs):
    q_refs, (k_ref, v_ref), outs = refs[:count], refs[count : count + 2], refs[count + 2 :]
    qrows = part

    def rows_at(ref, z, lo, hi):
        return ref[z, lo:hi] if len(ref.shape) == 3 else ref[z * qrows + lo : z * qrows + hi]

    part = part // local
    columns = steps * part
    qs = [
        jnp.concatenate(
            [
                rows_at(ref, z, kl * part, (kl + 1) * part)
                for ref in q_refs
                for z in range(steps)
            ], axis=0
        )
        for kl in range(local)
    ]
    heads = attend(qs, k_ref, v_ref, scale)
    for i in range(count):
        at = slice(i * columns, (i + 1) * columns)
        os, lses = zip(*((o[:, at], lse[:1, at]) for o, lse in heads))
        if own and i == count - 1:
            outs[i][...] = jnp.concatenate(os, axis=0)
            outs[i + 1][:local] = jnp.concatenate(lses, axis=0)
        else:
            outs[i][...] = encode(os, lses)


def join_partials_kernel(local, o_ref, lse_ref, other_ref, out_ref):
    size = o_ref.shape[0] // local
    parts = [
        merge([(o_ref[kl * size : (kl + 1) * size], lse_ref[kl : kl + 1]), other])
        for kl, other in enumerate(decode(other_ref[: out_ref.shape[0]], local))
    ]
    out_ref[...] = encode(*zip(*parts))


def near_kernel(count, size, local, group, scale, q_ref, fresh_ref, so_ref, sl_ref, po_ref, pl_ref, *refs):
    others, (out_ref, lse_ref) = refs[:count], refs[count:]
    nz, qrows = q_ref.shape[:2]
    part = qrows // local
    nb = part // group
    columns = nz * part
    head_dim = so_ref.shape[1]
    decoded = [decode(ref[ref.shape[0] - size :], local) for ref in others]
    for kl in range(local):
        scores, news = [], []
        for step in range(nz):
            q = q_ref[step, kl * part : (kl + 1) * part].astype(F32)
            tail = fresh_ref[step].astype(F32)
            k, v = (
                jnp.concatenate(
                    [
                        jnp.broadcast_to(tail[i : i + 1], (group, head_dim))
                        for i in range(at + kl * nb, at + (kl + 1) * nb)
                    ],
                    axis=0,
                )
                for at in (0, nb * local)
            )
            scores.append(jnp.sum(q * k, axis=1, keepdims=True) * scale)
            news.append(v)
        rows = slice(kl * columns, (kl + 1) * columns)
        out, lse = merge(
            [
                (jnp.concatenate(news, axis=0), jnp.concatenate(scores, axis=0)),
                (so_ref[rows], sl_ref[rows]),
            ]
        )
        at = slice(kl * head_dim, (kl + 1) * head_dim)
        parts = [(out.T, lse.T[:1]), (po_ref[at], pl_ref[kl : kl + 1])]
        out, lse = merge(parts + [d[kl] for d in decoded])
        out_ref[at] = out
        lse_ref[kl : kl + 1] = lse


def final_kernel(count, local, near_ref, lse_ref, *refs):
    others, outs = refs[:count], refs[count:]
    head_dim = near_ref.shape[0] // local
    part = outs[0].shape[0] // local
    decoded = [decode(ref[...], local) for ref in others]
    for kl in range(local):
        at = slice(kl * head_dim, (kl + 1) * head_dim)
        out, _ = merge([(near_ref[at], lse_ref[kl : kl + 1])] + [d[kl] for d in decoded])
        out = out.T
        for step, ref in enumerate(outs):
            ref[kl * part : (kl + 1) * part] = out[step * part : (step + 1) * part].astype(BF16)


def unpack_kernel(order, local, group, *refs):
    pieces, out_ref = refs[:-1], refs[-1]
    nz = len(order)
    me = lax.axis_index("branch")
    nb = out_ref.shape[0]
    for at, step in enumerate(order):
        peer = partner(me, step, nz)
        wide = pieces[at][...].astype(F32)
        for b in range(nb):
            rows = [wide[(kl * nb + b) * group : (kl * nb + b + 1) * group] for kl in range(local)]
            out_ref[b, peer] = jnp.concatenate(rows, axis=0).astype(BF16)


def per_device(
    nz, nblk, queries, new_keys, fresh_token_values, prefix_keys, prefix_values, suffix_keys,
    suffix_values, suffix_lengths, slot_branch
):
    nb, heads, head_dim = queries.shape
    positions, local = prefix_keys.shape[:2]
    group = heads // new_keys.shape[1]
    slots, suffix = suffix_keys.shape[:2]
    scale = 1.0 / math.sqrt(head_dim)
    qrows = local * nb * group
    used = qrows + 2 * nb * local
    padded = ceil_to(used, 16)
    rows = nz * qrows
    order = [*range(nz - 1, 0, -1), 0]
    nc = 2 if nblk % 2 == 0 else 1
    nx = nblk // nc

    def shift(x, axis, step, count):
        return lax.ppermute(x, axis, [(i, partner(i, step, count)) for i in range(count)])

    def along_blk(x, step_x, step_c):
        return lax.ppermute(
            x,
            "blk",
            [
                (i, partner(i // nc, step_x, nx) * nc + partner(i % nc, step_c, nc))
                for i in range(nblk)
            ],
        )

    payloads = call(
        functools.partial(pack_kernel, nz, local, group, padded - used),
        "pack",
        [pltpu.VMEM((padded, head_dim), BF16)] * nz,
        (
            in_hbm(queries.reshape(nb, nz, heads // nz, head_dim)),
            in_hbm(new_keys), in_hbm(fresh_token_values),
        ),
        [HBM] * 3,
        scratch=[
            pltpu.VMEM((nb, nz, heads // nz, head_dim), BF16),
            pltpu.VMEM(new_keys.shape, BF16),
            pltpu.VMEM(new_keys.shape, BF16),
            pltpu.SemaphoreType.DMA((nb + 2,)),
        ],
        moved=queries.size * 4,
    )
    gap = call(
        gap_kernel, "gap", pltpu.VMEM((8, head_dim), F32), (payloads[0],), [VM], flops=GAP, moved=GAP,
    )
    payloads, gap = lax.optimization_barrier((payloads, gap))
    arrived = [payloads[0]] + [
        shift(payloads[step], "branch", step, nz) for step in range(nz - 1, 0, -1)
    ][::-1]
    chunk = math.gcd(positions * local, 1024)
    flat = (positions * local, head_dim)
    width = suffix * local
    slot_rows = (slots, width, head_dim)
    slot_keys, slot_values = suffix_keys.reshape(slot_rows), suffix_values.reshape(slot_rows)
    keys, values, token = call(
        functools.partial(split_kernel, local),
        "split",
        [pltpu.VMEM((local, positions, head_dim), BF16)] * 2 + [pltpu.VMEM((8, head_dim), F32)],
        (prefix_keys.reshape(flat), prefix_values.reshape(flat)),
        [VM] * 2,
        scratch=[pltpu.VMEM((chunk, head_dim), F32)],
        vmem=8 << 20,
        moved=prefix_keys.size * 8,
    )
    joined, fresh = call(
        functools.partial(join_kernel, order, qrows),
        "join",
        [
            jax.ShapeDtypeStruct((nz, qrows, head_dim), BF16),
            jax.ShapeDtypeStruct((nz, padded - qrows, head_dim), BF16),
        ],
        (*[arrived[step] for step in order], gap, token),
        [VM] * (nz + 2),
        moved=nz * padded * head_dim * 4,
    )

    columns = rows // local
    state = [
        jax.ShapeDtypeStruct((local * head_dim, columns), F32),
        jax.ShapeDtypeStruct((ceil_to(local, 8), columns), F32),
    ]
    payload = jax.ShapeDtypeStruct((local * head_dim + ceil_to(3 * local, 16), columns), BF16)

    bundle = jax.ShapeDtypeStruct((rows + payload.shape[0], head_dim), BF16)

    def prefix(name, arrays, own=False):
        count = len(arrays)
        return call(
            functools.partial(prefix_kernel, count, own, nz, local, qrows, scale),
            name,
            [payload] * (count - own) + (state if own else []),
            (*arrays, keys, values),
            [VM] * (count + 2),
            vmem=16 << 20,
            flops=4 * count * rows * positions * head_dim,
            moved=4 * keys.size,
        )

    near_steps = [(0, c) for c in range(1, nc)]
    arriving = {
        step: along_blk(joined, *step) for step in [(x, nc - 1) for x in range(1, nx)] + near_steps
    }

    def give_back(x, step):
        return along_blk(x, back(step[0], nx), back(step[1], nc))

    rows_of = [arriving[step] for step in near_steps]
    *sibling, own_out, own_lse = prefix("prefix_near", [*rows_of, joined], own=True)
    distant = []
    returned = False
    for far in range(1, nx):
        rows_of, own_lse = lax.optimization_barrier((arriving[far, nc - 1], own_lse))
        (sent,) = prefix("prefix_far", [rows_of])
        if nc > 1:
            hopped = give_back(sent, (0, 1))
            queries_of = arriving[far, nc - 1]
            if far == 1 and columns == head_dim:
                queries_of = call(
                    bundle_kernel, "bundle", bundle, (queries_of, *sibling), [VM] * 2
                )
            queries_of = along_blk(queries_of, 0, 1)
            if far == 1 and columns == head_dim:
                sibling = [queries_of]
                returned = True
            rows_of, own_lse = lax.optimization_barrier((queries_of, own_lse))
            rows_of, sent = lax.optimization_barrier((rows_of, sent))
            partial = prefix("prefix_x", [rows_of], own=True)
            sent = call(
                functools.partial(join_partials_kernel, local),
                "join_partials",
                payload,
                (*partial, hopped),
                [VM] * 3,
            )
        distant.append(give_back(sent, (far, 0)))
        sent, own_lse = lax.optimization_barrier((sent, own_lse))
    if not returned:
        sibling = [give_back(x, step) for x, step in zip(sibling, near_steps)]
    own_lse, slot_keys = lax.optimization_barrier((own_lse, slot_keys))
    suffix_state = call(
        functools.partial(suffix_kernel, nz, local, group, scale),
        "suffix",
        [jax.ShapeDtypeStruct((rows, head_dim), F32)] * 2,
        (joined, slot_branch, suffix_lengths, slot_keys, slot_values),
        [VM, SM, SM, VM, VM],
        scratch=[
            pltpu.VMEM((rows, head_dim), F32),
            pltpu.VMEM((slots * local * group, width), F32),
            pltpu.VMEM((slots * local * group, width), BF16),
        ],
        vmem=8 << 20,
    )
    near = call(
        functools.partial(near_kernel, len(sibling), payload.shape[0], local, group, scale),
        "near",
        state,
        (joined, fresh, *suffix_state, own_out, own_lse, *sibling),
        [VM] * (6 + len(sibling)),
        moved=rows * head_dim * 20,
    )
    pieces = call(
        functools.partial(final_kernel, len(distant), local),
        "final",
        [jax.ShapeDtypeStruct((qrows, head_dim), BF16)] * nz,
        (*near, *distant),
        [VM] * (2 + len(distant)),
        moved=rows * head_dim * 20,
    )
    landed = [pieces[0]] + [
        shift(pieces[step], "branch", back(step, nz), nz) for step in range(nz - 1, 0, -1)
    ][::-1]
    out = call(
        functools.partial(unpack_kernel, order, local, group),
        "unpack",
        jax.ShapeDtypeStruct((nb, nz, heads // nz, head_dim), BF16),
        [landed[step] for step in order],
        [VM] * nz,
        moved=queries.size * 4,
    )
    return out.reshape(nb, heads, head_dim)


def solution(mesh):
    lanes = P(("groups", "blk", "branch"), None, None)
    return jax.shard_map(
        functools.partial(per_device, mesh.shape["branch"], mesh.shape["blk"]),
        mesh=mesh,
        in_specs=(
            lanes,
            lanes,
            lanes,
            P(("groups", "blk"), "branch", None),
            P(("groups", "blk"), "branch", None),
            P(("groups", "blk"), None, "branch", None),
            P(("groups", "blk"), None, "branch", None),
            P("groups"),
            P("groups"),
        ),
        out_specs=lanes,
        check_vma=False,
    )
```
